512 devices in a mesh: tile: 32 (over z, core), band: 4 (over x), pos: 4 (over y).
Axes of the slice: x: 4, y: 4, z: 16, core: 2. Of those that a mesh axis runs over, the one named last changes fastest.
Arguments:
- object_planes: float32 [2, 8192, 1024], P(None, 'tile', 'band'), may hold values from -6 to 6
- probe_planes: float32 [2, 2, 256, 256], replicated, may hold values from -6 to 6
- patterns: float32 [32, 4, 4, 3, 256, 256], P('tile', 'band', 'pos'), may hold values from 0.5 to 8
- offsets: int32 [32, 4, 4, 3, 2], P('tile', 'band', 'pos'), may hold values from 0 to 255, as said below
- counts: int32 [32, 4, 4], P('tile', 'band', 'pos'), may hold values from 0 to 3, as said below
Outputs:
- object_new: float32 [2, 8192, 1024], P(None, 'tile', 'band')
- probe_new: float32 [2, 2, 256, 256], replicated
The draws below stay inside these ranges and needn't reach their ends.
Inputs may be any that keep to these rules, and one draw needn't show every extreme that they name: `offsets`: corners lie inside their tile: rows below 256, columns below 256. Only the first counts[t, b, p] slots of a device hold positions; later slots are to be ignored. `counts`: each device holds at most 3 positions; in every tile one device along pos holds exactly 3, and the 4 devices of a tile hold exactly 8 positions together.
All inputs are finite; a program needn't handle non-finite values.
Results may differ from the reference program's by a relative error of at most 0.0003.
Values sent between devices are 32-bit elements; how exact they have to be, the bound alone decides.
No kernel may reach another device: no remote copies, remote signals or barrier semaphores. Data moves between devices by JAX's collectives and lax.ppermute only.
A program may use at most 192 MiB of HBM per device.

```python
import math
from functools import partial
import jax
import jax.numpy as jnp
from jax import lax

S = 256
MODES = 2
CAP = 3
BAL = 2
TR = 256
TC = 256
OBJ_ROWS = 8192
OBJ_COLS = 1024
N_TILE = 32
N_BAND = 4
N_POS = 4


def draw_offsets(key, part):
    key = jax.random.fold_in(key, 5)
    row_key, col_key = jax.random.split(key)
    shape_rows = (N_TILE, N_BAND, N_POS, CAP, 1)
    rows_drawn = jax.random.randint(row_key, shape_rows, 0, TR, dtype=jnp.int32)
    cols_drawn = jax.random.randint(col_key, shape_rows, 0, TC, dtype=jnp.int32)
    return jnp.concatenate([rows_drawn, cols_drawn], axis=-1)


def draw_counts(key, part):
    key = jax.random.fold_in(key, 9)
    first_key, second_key, third_key = jax.random.split(key, 3)
    regions = N_TILE * N_BAND
    remaining = BAL * N_POS - CAP
    count_one = jax.random.randint(first_key, (regions,), 0, CAP + 1, dtype=jnp.int32)
    lower = jnp.maximum(0, remaining - CAP - count_one)
    upper = jnp.minimum(CAP, remaining - count_one)
    count_two = jax.random.randint(second_key, (regions,), lower, upper + 1, dtype=jnp.int32)
    count_three = remaining - count_one - count_two
    full_count = jnp.full((regions,), CAP, jnp.int32)
    base_counts = jnp.stack([full_count, count_one, count_two, count_three], axis=-1)
    scores = jax.random.randint(third_key, (regions, 4), 0, 1 << 20, dtype=jnp.int32) * 4 + jnp.arange(4, dtype=jnp.int32)
    ordering = jnp.argsort(scores, axis=-1, stable=True)
    return jnp.take_along_axis(base_counts, ordering, axis=-1).reshape(N_TILE, N_BAND, N_POS)


def block_levels(rng, dims, pieces, smallest, high):
    loudness, own = 1.0, jax.random.fold_in(rng, 6)
    for axis_at, shards_of in pieces:
        heights = jnp.exp(jax.random.uniform(jax.random.fold_in(own, axis_at), (shards_of,), jnp.float32, smallest / len(pieces), high / len(pieces)))
        loudness = loudness * jnp.repeat(heights, dims[axis_at] // shards_of).reshape([-1 if axis == axis_at else 1 for axis in range(len(dims))])
    return loudness


def centred(rng, dims, width, limit, shards=(), held_as=jnp.bfloat16):
    array = width * jax.random.normal(rng, dims, jnp.float32)
    if shards:
        array = array * block_levels(rng, dims, shards, -0.22, 0.18)
    return jnp.clip(array, -limit, limit).astype(held_as)


def setup_inputs(seed: int = 0) -> dict:
    key_of = jax.random.split(jax.random.key(seed), 6)
    object_planes = centred(key_of[0], (2, OBJ_ROWS, OBJ_COLS), 1.0, 6.0, ((1, 32), (2, 4)), jnp.float32)
    probe_planes = centred(key_of[1], (2, MODES, S, S), 1.0, 6.0, (), jnp.float32)
    patterns = jnp.clip(jnp.exp(math.log(8.0) - 2.7725887 * jax.random.uniform(key_of[2], (N_TILE, N_BAND, N_POS, CAP, S, S), jnp.float32) ** block_levels(key_of[2], (N_TILE, N_BAND, N_POS, CAP, S, S), ((0, 32), (1, 4), (2, 4)), -0.2, 0.2)), 0.5, 8.0)
    offsets = draw_offsets(jax.random.fold_in(key_of[5], 71), 0)
    counts = draw_counts(jax.random.fold_in(key_of[5], 71), 0)
    return {"object_planes": object_planes, "probe_planes": probe_planes, "patterns": patterns, "offsets": offsets, "counts": counts}


def one_position(extended, probe_field, probe_power, measured, corner, weight):
    zero_index = jnp.int32(0)
    window = lax.dynamic_slice(extended, (zero_index, corner[0], corner[1]), (2, S, S))
    patch_field = window[0] + 1j * window[1]
    exit_wave = probe_field * patch_field[None]
    far_field = jnp.fft.fft2(exit_wave, norm='ortho')
    intensity = lax.optimization_barrier(jnp.sum(jnp.real(far_field) ** 2 + jnp.imag(far_field) ** 2, axis=0))
    scaling = jnp.sqrt(measured) / jnp.sqrt(intensity + 1.0)
    correction = jnp.fft.ifft2(far_field * scaling[None], norm='ortho') - exit_wave
    object_term = weight * lax.optimization_barrier(jnp.sum(jnp.conj(probe_field) * correction, axis=0))
    contribution = jnp.stack([jnp.real(object_term), jnp.imag(object_term), weight * probe_power])
    probe_term = weight * jnp.conj(patch_field)[None] * correction
    density = weight * (window[0] ** 2 + window[1] ** 2)
    return (contribution, jnp.real(probe_term), jnp.imag(probe_term), density)

def reference(object_planes, probe_planes, patterns, offsets, counts):
    padded = jnp.pad(object_planes, ((0, 0), (0, S), (0, S)))
    probe_field = probe_planes[0] + 1j * probe_planes[1]
    probe_power = lax.optimization_barrier(jnp.sum(probe_planes[0] ** 2 + probe_planes[1] ** 2, axis=0))
    slot_index = jnp.arange(CAP, dtype=jnp.int32)
    zero_index = jnp.int32(0)

    def one_region(totals, region_index):
        object_sum, probe_real, probe_imag, density_sum = totals
        tile_at = region_index // N_BAND
        band_at = region_index % N_BAND
        row_first = tile_at * TR
        col_first = band_at * TC
        extended = lax.dynamic_slice(padded, (zero_index, row_first, col_first), (2, TR + S, TC + S))
        region_frames = lax.dynamic_slice(patterns, (tile_at, band_at, zero_index, zero_index, zero_index, zero_index), (1, 1, N_POS, CAP, S, S)).reshape(N_POS * CAP, S, S)
        region_corners = lax.dynamic_slice(offsets, (tile_at, band_at, zero_index, zero_index, zero_index), (1, 1, N_POS, CAP, 2)).reshape(N_POS * CAP, 2)
        region_counts = lax.dynamic_slice(counts, (tile_at, band_at, zero_index), (1, 1, N_POS)).reshape(N_POS)
        alive_mask = (slot_index[None, :] < region_counts[:, None]).reshape(N_POS * CAP).astype(object_planes.dtype)
        worker = partial(one_position, extended, probe_field, probe_power)
        contributions, term_real, term_imag, densities = jax.vmap(worker)(region_frames, region_corners, alive_mask)

        def add_patch(number, running):
            corner = region_corners[number]
            previous = lax.dynamic_slice(running, (zero_index, corner[0], corner[1]), (3, S, S))
            return lax.dynamic_update_slice(running, previous + contributions[number], (zero_index, corner[0], corner[1]))
        local_sum = lax.fori_loop(0, N_POS * CAP, add_patch, jnp.zeros((3, TR + S, TC + S), object_planes.dtype))
        current = lax.dynamic_slice(object_sum, (zero_index, row_first, col_first), (3, TR + S, TC + S))
        object_sum = lax.dynamic_update_slice(object_sum, current + local_sum, (zero_index, row_first, col_first))
        new_totals = (object_sum, probe_real + lax.optimization_barrier(jnp.sum(term_real, axis=0)), probe_imag + lax.optimization_barrier(jnp.sum(term_imag, axis=0)), density_sum + lax.optimization_barrier(jnp.sum(densities, axis=0)))
        return (new_totals, None)
    starting = (jnp.zeros((3, OBJ_ROWS + S, OBJ_COLS + S), object_planes.dtype), jnp.zeros((MODES, S, S), object_planes.dtype), jnp.zeros((MODES, S, S), object_planes.dtype), jnp.zeros((S, S), object_planes.dtype))
    finals, unused = lax.scan(one_region, starting, jnp.arange(N_TILE * N_BAND, dtype=jnp.int32))
    object_sum, probe_real, probe_imag, density_sum = finals
    cropped = object_sum[:, :OBJ_ROWS, :OBJ_COLS]
    object_new = object_planes + cropped[:2] / (cropped[2] + 1.0)
    probe_new = probe_planes + jnp.stack([probe_real, probe_imag]) / (density_sum + 1.0)
    return (object_new, probe_new)
```

```python
import functools
import math

import jax
import jax.numpy as jnp
import ml_dtypes
import numpy as np
from jax import lax
from jax.experimental import pallas as pl
from jax.experimental.pallas import tpu as pltpu
from jax.sharding import PartitionSpec as P

S = 256
QUARTERS = 4


def tables():
    index = np.arange(S)
    angle = (index[:, None] * index[None, :] % S) * (2.0 * math.pi / S)
    cosine, sine = np.cos(angle) / 16.0, np.sin(angle) / 16.0
    left = np.block([[cosine, sine], [-sine, cosine]]).astype(np.float32)
    head = left.astype(ml_dtypes.bfloat16)
    rest = (left - head.astype(np.float32)).astype(ml_dtypes.bfloat16)
    return (head, rest, np.ascontiguousarray(head.T), np.ascontiguousarray(rest.T))


def split(value):
    head = value.astype(jnp.bfloat16)
    return head, (value - head.astype(jnp.float32)).astype(jnp.bfloat16)


def product(first, second):
    dot = functools.partial(jnp.dot, preferred_element_type=jnp.float32)
    return dot(first[0], second[0]) + dot(first[0], second[1]) + dot(first[1], second[0])


def regroup(value):
    return jnp.concatenate(
        [
            jnp.concatenate([value[:S, :S], value[S:, :S]], axis=1),
            jnp.concatenate([value[:S, S:], value[S:, S:]], axis=1),
        ],
        axis=0,
    )


def cut(block, row, column):
    block = pltpu.roll(block, lax.rem(2 * S - column, 2 * S), 1)[:, :S]
    return pltpu.roll(block, lax.rem(S + 8 - row, S + 8), 0)[:S]


def placed(value, row, column):
    value = jnp.concatenate([value, jnp.zeros((8, S), jnp.float32)], axis=0)
    value = pltpu.roll(value, row, 0)
    return pltpu.roll(jnp.concatenate([value, jnp.zeros_like(value)], axis=1), column, 1)


def slots_kernel(
    places, scalars, own, right, below, corner, probe, frames, lh, lr, rh, rr,
    top_left, bottom_left, right_half, keep, send, extended, total, terms,
):
    extended[:, :S, :S] = own[...]
    extended[:, :S, S:] = right[...]
    extended[:, S:, :S] = below[...]
    extended[:, S:, S:] = corner[...]
    total[...] = jnp.zeros_like(total)
    terms[...] = jnp.zeros_like(terms)
    blank = jnp.zeros((S, S), jnp.float32)

    def one_slot(slot, carry):
        row, column = places[slot, 0], places[slot, 1]
        inside = lax.rem(row, 8)
        band_rows = pl.ds(pl.multiple_of(row - inside, 8), S + 8)
        patch_real, patch_imag = (cut(extended[p, band_rows, :], inside, column) for p in range(2))
        real = jnp.concatenate(
            [probe[0, m] * patch_real - probe[1, m] * patch_imag for m in range(2)], axis=1
        )
        imag = jnp.concatenate(
            [probe[0, m] * patch_imag + probe[1, m] * patch_real for m in range(2)], axis=1
        )
        left_table, right_table = (lh[...], lr[...]), (rh[...], rr[...])
        wave = product(left_table, split(jnp.concatenate([real, imag], axis=0)))
        far = product(split(regroup(wave)), right_table)
        power = far * far
        power = power[:S, :S] + power[:S, S:] + power[S:, :S] + power[S:, S:]
        change = jnp.sqrt(frames[slot]) / jnp.sqrt(power + 1.0) - 1.0
        swapped = jnp.concatenate(
            [
                jnp.concatenate([far[:S, S:] * change, far[:S, :S] * change], axis=1),
                jnp.concatenate([far[S:, S:] * change, far[S:, :S] * change], axis=1),
            ],
            axis=0,
        )
        back = product(split(swapped), right_table)
        chi = product(left_table, split(regroup(back)))
        object_real, object_imag = blank, blank
        for m in range(2):
            chi_imag = chi[:S, m * S : (m + 1) * S]
            chi_real = chi[S:, m * S : (m + 1) * S]
            object_real += probe[0, m] * chi_real + probe[1, m] * chi_imag
            object_imag += probe[0, m] * chi_imag - probe[1, m] * chi_real
            terms[m] += patch_real * chi_real + patch_imag * chi_imag
            terms[2 + m] += patch_real * chi_imag - patch_imag * chi_real
        terms[4] += patch_real * patch_real + patch_imag * patch_imag
        light = jnp.zeros((S, S), jnp.float32)
        for m in range(2):
            light += probe[0, m] * probe[0, m] + probe[1, m] * probe[1, m]
        for plane, value in enumerate((object_real, object_imag, light)):
            total[plane, band_rows, :] += placed(value, inside, column)
        return carry

    lax.fori_loop(0, scalars[0], one_slot, 0)
    rows = S // QUARTERS
    for q in range(QUARTERS):
        for plane in range(3):
            at = q * rows
            top_left[q, plane] = total[plane, at : at + rows, :S]
            bottom_left[q, plane] = total[plane, S + at : S + at + rows, :S]
            right_half[0, q, plane] = total[plane, at : at + rows, S:]
            right_half[1, q, plane] = total[plane, S + at : S + at + rows, S:]
    chunks, _, height, _ = keep.shape
    core = scalars[1]
    for chunk in range(chunks):
        mine = pl.multiple_of(core * (S // 2) + chunk * height, height)
        other = pl.multiple_of((1 - core) * (S // 2) + chunk * height, height)
        for plane in range(5):
            keep[chunk, plane] = terms[plane, pl.ds(mine, height), :]
            send[chunk, plane] = terms[plane, pl.ds(other, height), :]


def run_slots(places, scalars, blocks, probe, frames, chunks):
    height = S // 2 // chunks
    f32 = jnp.float32
    quarter = (QUARTERS, 3, S // QUARTERS, S)
    vmem = pl.BlockSpec(memory_space=pltpu.VMEM)
    smem = pl.BlockSpec(memory_space=pltpu.SMEM)
    return pl.pallas_call(
        slots_kernel,
        out_shape=(
            jax.ShapeDtypeStruct(quarter, f32),
            jax.ShapeDtypeStruct(quarter, f32),
            jax.ShapeDtypeStruct((2, *quarter), f32),
            jax.ShapeDtypeStruct((chunks, 5, height, S), f32),
            jax.ShapeDtypeStruct((chunks, 5, height, S), f32),
        ),
        in_specs=[smem] * 2 + [vmem] * 10,
        out_specs=[vmem] * 5,
        scratch_shapes=[
            pltpu.VMEM((2, 2 * S, 2 * S), f32),
            pltpu.VMEM((3, 2 * S, 2 * S), f32),
            pltpu.VMEM((5, S, S), f32),
        ],
        compiler_params=pltpu.CompilerParams(vmem_limit_bytes=52 * 1024 * 1024),
        name="slots",
    )(places, scalars, *blocks, probe, frames, *(jnp.asarray(t) for t in tables()))


def shifted(block, axis, distance):
    devices = range(lax.axis_size(axis))
    route = [(i - distance, i) for i in devices if i - distance in devices]
    return lax.ppermute(block, axis, route)


def crossed(block, bit):
    devices = range(lax.axis_size("tile"))
    return lax.ppermute(block, "tile", [(i, i ^ bit) for i in devices])


def exchanged(block, axes):
    return lax.all_to_all(block, axes, 0, 0)


def on_device(object_planes, probe_planes, patterns, offsets, counts):
    core = lax.axis_index("tile") % 2
    plane = ("band", "pos")
    chunks = lax.axis_size("band") * lax.axis_size("pos")
    right = shifted(object_planes, "band", -1)
    below = shifted(object_planes, "tile", -1)
    corner = shifted(right, "tile", -1)
    scalars = jnp.stack([counts.reshape(()), core.astype(jnp.int32)])
    top, bottom, right_half, keep, send = run_slots(
        offsets[0, 0, 0], scalars, (object_planes, right, below, corner),
        probe_planes, patterns[0, 0, 0], chunks,
    )

    from_left = shifted(right_half, "band", 1)
    terms = keep + crossed(send, 1)
    from_above = shifted(bottom + from_left[1], "tile", 1)
    terms = jnp.sum(exchanged(terms, plane), axis=0)
    tile_sum = top + from_left[0] + from_above
    tile_sum = jnp.sum(exchanged(tile_sum, "pos"), axis=0)
    bit = 2
    while bit < lax.axis_size("tile"):
        terms = terms + crossed(terms, bit)
        bit *= 2

    rows = S // QUARTERS
    own_rows = lax.dynamic_slice_in_dim(object_planes, lax.axis_index("pos") * rows, rows, 1)
    own_rows = own_rows + tile_sum[:2] / (tile_sum[2] + 1.0)
    gathered = exchanged(jnp.broadcast_to(own_rows, (QUARTERS, *own_rows.shape)), "pos")
    object_new = gathered.transpose(1, 0, 2, 3).reshape(object_planes.shape)

    height = S // 2 // chunks
    place = core * (S // 2) + (lax.axis_index("band") * lax.axis_size("pos") + lax.axis_index("pos")) * height
    own_probe = lax.dynamic_slice_in_dim(probe_planes.reshape(4, S, S), place, height, 1)
    own_probe = own_probe + terms[:4] / (terms[4] + 1.0)
    mine = exchanged(jnp.broadcast_to(own_probe, (chunks, *own_probe.shape)), plane)
    other = crossed(mine, 1)
    halves = jnp.stack(
        [jnp.where(core == 0, mine, other), jnp.where(core == 0, other, mine)]
    )
    probe_new = halves.transpose(2, 0, 1, 3, 4).reshape(probe_planes.shape)
    return (object_new, probe_new)


def solution(mesh):
    in_specs = (
        P(None, "tile", "band"),
        P(),
        P("tile", "band", "pos", None, None, None),
        P("tile", "band", "pos", None, None),
        P("tile", "band", "pos"),
    )
    out_specs = (P(None, "tile", "band"), P())
    return jax.shard_map(
        on_device, mesh=mesh, in_specs=in_specs, out_specs=out_specs, check_vma=False
    )
```

```python
import functools
import math

import jax
import jax.numpy as jnp
import ml_dtypes
import numpy as np
from jax import lax
from jax.experimental import pallas as pl
from jax.experimental.pallas import tpu as pltpu
from jax.sharding import PartitionSpec as P

S = 256
QUARTERS = 4


def tables():
    index = np.arange(S)
    angle = (index[:, None] * index[None, :] % S) * (2.0 * math.pi / S)
    cosine, sine = np.cos(angle) / 16.0, np.sin(angle) / 16.0
    left = np.block([[cosine, sine], [-sine, cosine]]).astype(np.float32)
    head = left.astype(ml_dtypes.bfloat16)
    rest = (left - head.astype(np.float32)).astype(ml_dtypes.bfloat16)
    return (head, rest, np.ascontiguousarray(head.T), np.ascontiguousarray(rest.T))


def split(value):
    head = value.astype(jnp.bfloat16)
    return head, (value - head.astype(jnp.float32)).astype(jnp.bfloat16)


def product(first, second):
    dot = functools.partial(jnp.dot, preferred_element_type=jnp.float32)
    return dot(first[0], second[0]) + dot(first[0], second[1]) + dot(first[1], second[0])


def regroup(value):
    return jnp.concatenate(
        [
            jnp.concatenate([value[:S, :S], value[S:, :S]], axis=1),
            jnp.concatenate([value[:S, S:], value[S:, S:]], axis=1),
        ],
        axis=0,
    )


def cut(block, row, column):
    height = block.shape[0]
    lane = lax.broadcasted_iota(jnp.int32, (height, 128), 1)
    turned = [pltpu.roll(block[:, k * 128 : k * 128 + 128], 128 - column, 1) for k in range(3)]
    block = jnp.concatenate(
        [jnp.where(lane < 128 - column, turned[k], turned[k + 1]) for k in range(2)], axis=1
    )
    turned = pltpu.roll(block.reshape(height // 8, 8, S), 8 - row, 1)
    within = lax.broadcasted_iota(jnp.int32, (height // 8 - 1, 8, S), 1)
    return jnp.where(within < 8 - row, turned[:-1], turned[1:]).reshape(height - 8, S)


def placed(value, row, column):
    turned = pltpu.roll(value.reshape(S // 8, 8, S), row, 1)
    gap = jnp.zeros((1, 8, S), jnp.float32)
    within = lax.broadcasted_iota(jnp.int32, (S // 8 + 1, 8, S), 1)
    value = jnp.where(
        within < row, jnp.concatenate([gap, turned], axis=0), jnp.concatenate([turned, gap], axis=0)
    ).reshape(S + 8, S)
    lane = lax.broadcasted_iota(jnp.int32, (S + 8, 128), 1)
    turned = [pltpu.roll(value[:, k * 128 : k * 128 + 128], column, 1) for k in range(2)]
    return jnp.concatenate(
        [
            jnp.where(lane < column, 0.0, turned[0]),
            jnp.where(lane < column, turned[0], turned[1]),
            jnp.where(lane < column, turned[1], 0.0),
        ],
        axis=1,
    )


def slots_kernel(
    places, scalars, own, right, below, corner_a, corner_b, probe, frames, lh, lr, rh, rr, after,
    left_half, right_half, keep, send, extended, total, terms,
):
    extended[:, :S, :S] = own[...]
    extended[:, :S, S:] = right[...]
    extended[:, S:, :S] = below[...]
    extended[:, S:, S:] = corner_a[...] + corner_b[...]
    total[...] = jnp.zeros_like(total)
    terms[...] = jnp.zeros_like(terms)
    blank = jnp.zeros((S, S), jnp.float32)

    def one_slot(slot, carry):
        row, column = places[slot, 0], places[slot, 1]
        inside = lax.rem(row, 8)
        band_rows = pl.ds(pl.multiple_of(row - inside, 8), S + 8)
        fine = lax.rem(column, 128)
        band_columns = pl.ds(pl.multiple_of(column - fine, 128), 384)
        patch_real, patch_imag = (cut(extended[p, band_rows, band_columns], inside, fine) for p in range(2))
        left_table, right_table = (lh[...], lr[...]), (rh[...], rr[...])
        RC = 256
        wave = []
        for m in range(2):
            real = probe[0, m] * patch_real - probe[1, m] * patch_imag
            imag = probe[0, m] * patch_imag + probe[1, m] * patch_real
            wave.append(product(left_table, split(jnp.concatenate([real, imag], axis=0))))
        back = [[], []]
        for at in range(0, S, RC):
            part = slice(at, at + RC)
            far = [
                jnp.concatenate([wave[m][at : at + RC], wave[m][S + at : S + at + RC]], axis=1)
                for m in range(2)
            ]
            far = product(split(jnp.concatenate(far, axis=0)), right_table)
            power = far[:RC] * far[:RC] + far[RC:] * far[RC:]
            power = power[:, :S] + power[:, S:]
            change = jnp.sqrt(frames[slot, part]) / jnp.sqrt(power + 1.0) - 1.0
            change = jnp.concatenate([change, change], axis=0)
            swapped = jnp.concatenate([far[:, S:] * change, far[:, :S] * change], axis=1)
            chunk = product(split(swapped), right_table)
            for m in range(2):
                back[m].append(chunk[m * RC : m * RC + RC])
        object_real, object_imag = blank, blank
        for m in range(2):
            whole = jnp.concatenate([c[:, :S] for c in back[m]] + [c[:, S:] for c in back[m]], axis=0)
            chi = product(left_table, split(whole))
            chi_imag, chi_real = chi[:S], chi[S:]
            object_real += probe[0, m] * chi_real + probe[1, m] * chi_imag
            object_imag += probe[0, m] * chi_imag - probe[1, m] * chi_real
            terms[m] += patch_real * chi_real + patch_imag * chi_imag
            terms[2 + m] += patch_real * chi_imag - patch_imag * chi_real
        terms[4] += patch_real * patch_real + patch_imag * patch_imag
        for plane, value in enumerate((object_real, object_imag)):
            total[plane, band_rows, band_columns] += placed(value, inside, fine)
        return carry

    lax.fori_loop(0, scalars[0], one_slot, 0)
    left_half[...] = total[:, :, :S]
    right_half[...] = total[:, :, S:]
    chunks, _, height, _ = keep.shape
    core = scalars[1]
    for chunk in range(chunks):
        mine = pl.multiple_of(core * (S // 2) + chunk * height, height)
        other = pl.multiple_of((1 - core) * (S // 2) + chunk * height, height)
        for plane in range(5):
            keep[chunk, plane] = terms[plane, pl.ds(mine, height), :]
            send[chunk, plane] = terms[plane, pl.ds(other, height), :]


def run_slots(places, scalars, blocks, probe, frames, chunks, after):
    height = S // 2 // chunks
    f32 = jnp.float32
    vmem = pl.BlockSpec(memory_space=pltpu.VMEM)
    smem = pl.BlockSpec(memory_space=pltpu.SMEM)
    return pl.pallas_call(
        slots_kernel,
        out_shape=(
            jax.ShapeDtypeStruct((2, 2 * S, S), f32),
            jax.ShapeDtypeStruct((2, 2 * S, S), f32),
            jax.ShapeDtypeStruct((chunks, 5, height, S), f32),
            jax.ShapeDtypeStruct((chunks, 5, height, S), f32),
        ),
        in_specs=[smem] * 2 + [vmem] * 11 + [pl.BlockSpec(memory_space=pl.ANY)],
        out_specs=[vmem] * 4,
        scratch_shapes=[
            pltpu.VMEM((2, 2 * S, 2 * S), f32),
            pltpu.VMEM((2, 2 * S, 2 * S), f32),
            pltpu.VMEM((5, S, S), f32),
        ],
        compiler_params=pltpu.CompilerParams(vmem_limit_bytes=54 * 1024 * 1024),
        name="slots",
    )(places, scalars, *blocks, probe, frames, *(jnp.asarray(t) for t in tables()), after)


def light_kernel(gathered, scalars, probe, light, padded):
    power = jnp.zeros((S, S), jnp.float32)
    for m in range(2):
        power += probe[0, m] * probe[0, m] + probe[1, m] * probe[1, m]
    padded[...] = jnp.zeros_like(padded)
    padded[S : 2 * S, S : 2 * S] = power
    rows = S // QUARTERS
    band, quarter = scalars[2], scalars[3]
    posts = QUARTERS

    def one_device(number, sum_so_far):
        above, left, post = number // (2 * posts), (number // posts) % 2, number % posts
        source = jnp.maximum(band - left, 0) * posts + post
        live = jnp.where(band >= left, gathered[above, source, 6], 0)

        def one_position(slot, sum_so_far):
            first_row = S + quarter * rows + above * S - gathered[above, source, 2 * slot]
            first_column = S + left * S - gathered[above, source, 2 * slot + 1]
            inside, fine = lax.rem(first_row, 8), lax.rem(first_column, 128)
            block = padded[
                pl.ds(pl.multiple_of(first_row - inside, 8), rows + 8),
                pl.ds(pl.multiple_of(first_column - fine, 128), 384),
            ]
            return sum_so_far + cut(block, inside, fine)

        return lax.fori_loop(0, live, one_position, sum_so_far)

    light[...] = lax.fori_loop(0, 4 * posts, one_device, jnp.zeros((rows, S), jnp.float32))


def run_light(gathered, scalars, probe):
    vmem = pl.BlockSpec(memory_space=pltpu.VMEM)
    smem = pl.BlockSpec(memory_space=pltpu.SMEM)
    return pl.pallas_call(
        light_kernel,
        out_shape=jax.ShapeDtypeStruct((S // QUARTERS, S), jnp.float32),
        in_specs=[smem, smem, vmem],
        out_specs=vmem,
        scratch_shapes=[pltpu.VMEM((3 * S + 8, 3 * S + 128), jnp.float32)],
        compiler_params=pltpu.CompilerParams(vmem_limit_bytes=54 * 1024 * 1024),
        name="light",
    )(gathered, scalars, probe)


def shifted(block, axis, distance):
    devices = range(lax.axis_size(axis))
    route = [(i - distance, i) for i in devices if i - distance in devices]
    return lax.ppermute(block, axis, route)


def crossed(block, bit):
    devices = range(lax.axis_size("tile"))
    return lax.ppermute(block, "tile", [(i, i ^ bit) for i in devices])


def exchanged(block, axes):
    return lax.all_to_all(block, axes, 0, 0)


def shared(block, axes):
    return exchanged(jnp.broadcast_to(block, (lax.axis_size(axes), *block.shape)), axes)


def corners(right, below):
    tiles, bands = lax.axis_size("tile"), lax.axis_size("band")
    across = [(t * bands + b, t * bands + b - 1) for t in range(1, tiles, 2) for b in range(1, bands)]
    beside = [(t, t - 1) for t in range(1, tiles, 2)]
    return lax.ppermute(below, ("tile", "band"), across), lax.ppermute(right, "tile", beside)


def sum_along_z(block):
    bit, tiles = 2, lax.axis_size("tile")
    while bit < tiles:
        if 4 * bit <= tiles:
            one, two, three = (crossed(block, bit * k) for k in (1, 2, 3))
            block = (block + one) + (two + three)
            bit *= 4
        else:
            block = block + crossed(block, bit)
            bit *= 2
    return block


def on_device(object_planes, probe_planes, patterns, offsets, counts):
    core = lax.axis_index("tile") % 2
    band, post = lax.axis_index("band"), lax.axis_index("pos")
    bands, posts = lax.axis_size("band"), lax.axis_size("pos")
    plane = ("band", "pos")
    chunks = bands * posts
    right = shifted(object_planes, "band", -1)
    below = shifted(object_planes, "tile", -1)
    card = jnp.concatenate([offsets.reshape(6), counts.reshape(1), jnp.zeros(1, jnp.int32)])
    cards = shared(jnp.pad(card[None], ((0, 7), (0, 120))), plane)
    cards_above = shifted(cards, "tile", 1)
    corner_a, corner_b = corners(right, below)
    scalars = jnp.stack([counts.reshape(()), core, band, post])
    light = run_light(jnp.stack([cards[:, 0, :8], cards_above[:, 0, :8]]), scalars, probe_planes)
    left_half, right_half, keep, send = run_slots(
        offsets[0, 0, 0], scalars, (object_planes, right, below, corner_a, corner_b),
        probe_planes, patterns[0, 0, 0], chunks, light,
    )

    from_left = shifted(right_half, "band", 1)
    terms = keep + crossed(send, 1)
    terms = jnp.sum(exchanged(terms.reshape(posts, bands, *terms.shape[1:]), "pos"), axis=0)
    terms = jnp.sum(exchanged(terms, "band"), axis=0)
    merged = left_half + from_left
    from_above = shifted(merged[:, S:], "tile", 1)
    terms = sum_along_z(terms)

    rows = S // QUARTERS
    tile_sum = (merged[:, :S] + from_above).reshape(2, QUARTERS, rows, S).transpose(1, 0, 2, 3)
    tile_sum = jnp.sum(exchanged(tile_sum, "pos"), axis=0)
    own_rows = lax.dynamic_slice_in_dim(object_planes, post * rows, rows, 1)
    own_rows = own_rows + tile_sum / (light + 1.0)
    object_new = shared(own_rows, "pos").transpose(1, 0, 2, 3).reshape(object_planes.shape)

    height = S // 2 // chunks
    place = core * (S // 2) + (post * bands + band) * height
    own_probe = lax.dynamic_slice_in_dim(probe_planes.reshape(4, S, S), place, height, 1)
    own_probe = own_probe + terms[:4] / (terms[4] + 1.0)
    mine = shared(own_probe, plane)
    other = crossed(mine, 1)
    halves = jnp.stack(
        [jnp.where(core == 0, mine, other), jnp.where(core == 0, other, mine)]
    )
    halves = halves.reshape(2, bands, posts, 4, height, S).transpose(3, 0, 2, 1, 4, 5)
    probe_new = halves.reshape(probe_planes.shape)
    return (object_new, probe_new)


def solution(mesh):
    in_specs = (
        P(None, "tile", "band"),
        P(),
        P("tile", "band", "pos", None, None, None),
        P("tile", "band", "pos", None, None),
        P("tile", "band", "pos"),
    )
    out_specs = (P(None, "tile", "band"), P())
    return jax.shard_map(
        on_device, mesh=mesh, in_specs=in_specs, out_specs=out_specs, check_vma=False
    )
```

```python
import functools
import math

import jax
import jax.numpy as jnp
import ml_dtypes
import numpy as np
from jax import lax
from jax.experimental import pallas as pl
from jax.experimental.pallas import tpu as pltpu
from jax.sharding import PartitionSpec as P

S = 256
QUARTERS = 4
COUNT = 6
TILE = ("z_high", "z_low", "core")


def tables():
    index = np.arange(S)
    angle = (index[:, None] * index[None, :] % S) * (2.0 * math.pi / S)
    cosine, sine = np.cos(angle) / 16.0, np.sin(angle) / 16.0
    left = np.block([[cosine, sine], [-sine, cosine]]).astype(np.float32)
    head = left.astype(ml_dtypes.bfloat16)
    rest = (left - head.astype(np.float32)).astype(ml_dtypes.bfloat16)
    return (head, rest, np.ascontiguousarray(head.T), np.ascontiguousarray(rest.T))


def split(value):
    head = value.astype(jnp.bfloat16)
    return head, (value - head.astype(jnp.float32)).astype(jnp.bfloat16)


def product(first, second):
    dot = functools.partial(jnp.dot, preferred_element_type=jnp.float32)
    return dot(first[0], second[0]) + dot(first[0], second[1]) + dot(first[1], second[0])


def regroup(value):
    return jnp.concatenate(
        [
            jnp.concatenate([value[:S, :S], value[S:, :S]], axis=1),
            jnp.concatenate([value[:S, S:], value[S:, S:]], axis=1),
        ],
        axis=0,
    )


def cut(block, row, column):
    height = block.shape[0]
    lane = lax.broadcasted_iota(jnp.int32, (height, 128), 1)
    turned = [pltpu.roll(block[:, k * 128 : k * 128 + 128], 128 - column, 1) for k in range(3)]
    block = jnp.concatenate(
        [jnp.where(lane < 128 - column, turned[k], turned[k + 1]) for k in range(2)], axis=1
    )
    turned = pltpu.roll(block.reshape(height // 8, 8, S), 8 - row, 1)
    within = lax.broadcasted_iota(jnp.int32, (height // 8 - 1, 8, S), 1)
    return jnp.where(within < 8 - row, turned[:-1], turned[1:]).reshape(height - 8, S)


def placed(value, row, column):
    turned = pltpu.roll(value.reshape(S // 8, 8, S), row, 1)
    gap = jnp.zeros((1, 8, S), jnp.float32)
    within = lax.broadcasted_iota(jnp.int32, (S // 8 + 1, 8, S), 1)
    value = jnp.where(
        within < row, jnp.concatenate([gap, turned], axis=0), jnp.concatenate([turned, gap], axis=0)
    ).reshape(S + 8, S)
    lane = lax.broadcasted_iota(jnp.int32, (S + 8, 128), 1)
    turned = [pltpu.roll(value[:, k * 128 : k * 128 + 128], column, 1) for k in range(2)]
    return jnp.concatenate(
        [
            jnp.where(lane < column, 0.0, turned[0]),
            jnp.where(lane < column, turned[0], turned[1]),
            jnp.where(lane < column, turned[1], 0.0),
        ],
        axis=1,
    )


def slots_kernel(
    card, own, right, below, corner_a, corner_b, probe, frames, lh, lr, rh, rr, after,
    top_left, top_right, bottom, keep, send, extended, total, terms,
):
    extended[:, :S, :S] = own[...]
    extended[:, :S, S:] = right[...]
    extended[:, S:, :S] = below[...]
    extended[:, S:, S:] = corner_a[...] + corner_b[...]
    total[...] = jnp.zeros_like(total)
    terms[...] = jnp.zeros_like(terms)
    blank = jnp.zeros((S, S), jnp.float32)

    def one_slot(slot, carry):
        row, column = card[0, 2 * slot], card[0, 2 * slot + 1]
        inside = lax.rem(row, 8)
        band_rows = pl.ds(pl.multiple_of(row - inside, 8), S + 8)
        fine = lax.rem(column, 128)
        band_columns = pl.ds(pl.multiple_of(column - fine, 128), 384)
        patch_real, patch_imag = (cut(extended[p, band_rows, band_columns], inside, fine) for p in range(2))
        left_table, right_table = (lh[...], lr[...]), (rh[...], rr[...])
        RC = 256
        wave = []
        for m in range(2):
            real = probe[0, m] * patch_real - probe[1, m] * patch_imag
            imag = probe[0, m] * patch_imag + probe[1, m] * patch_real
            wave.append(product(left_table, split(jnp.concatenate([real, imag], axis=0))))
        back = [[], []]
        for at in range(0, S, RC):
            part = slice(at, at + RC)
            far = [
                jnp.concatenate([wave[m][at : at + RC], wave[m][S + at : S + at + RC]], axis=1)
                for m in range(2)
            ]
            far = product(split(jnp.concatenate(far, axis=0)), right_table)
            power = far[:RC] * far[:RC] + far[RC:] * far[RC:]
            power = power[:, :S] + power[:, S:]
            change = jnp.sqrt(frames[slot, part]) / jnp.sqrt(power + 1.0) - 1.0
            change = jnp.concatenate([change, change], axis=0)
            swapped = jnp.concatenate([far[:, S:] * change, far[:, :S] * change], axis=1)
            chunk = product(split(swapped), right_table)
            for m in range(2):
                back[m].append(chunk[m * RC : m * RC + RC])
        object_real, object_imag = blank, blank
        for m in range(2):
            whole = jnp.concatenate([c[:, :S] for c in back[m]] + [c[:, S:] for c in back[m]], axis=0)
            chi = product(left_table, split(whole))
            chi_imag, chi_real = chi[:S], chi[S:]
            object_real += probe[0, m] * chi_real + probe[1, m] * chi_imag
            object_imag += probe[0, m] * chi_imag - probe[1, m] * chi_real
            terms[m] += patch_real * chi_real + patch_imag * chi_imag
            terms[2 + m] += patch_real * chi_imag - patch_imag * chi_real
        terms[4] += patch_real * patch_real + patch_imag * patch_imag
        for plane, value in enumerate((object_real, object_imag)):
            total[plane, band_rows, band_columns] += placed(value, inside, fine)
        return carry

    lax.fori_loop(0, card[0, COUNT], one_slot, 0)
    rows = S // QUARTERS
    for q in range(QUARTERS):
        upper, lower = slice(q * rows, (q + 1) * rows), slice(S + q * rows, S + (q + 1) * rows)
        top_left[q] = total[:, upper, :S]
        top_right[q] = total[:, upper, S:]
        bottom[0, q] = total[:, lower, :S]
        bottom[1, q] = total[:, lower, S:]
    chunks, _, height, _ = keep.shape
    core = lax.axis_index("core")
    for chunk in range(chunks):
        mine = pl.multiple_of(core * (S // 2) + chunk * height, height)
        other = pl.multiple_of((1 - core) * (S // 2) + chunk * height, height)
        for plane in range(5):
            keep[chunk, plane] = terms[plane, pl.ds(mine, height), :]
            send[chunk, plane] = terms[plane, pl.ds(other, height), :]


def run_slots(card, blocks, probe, frames, chunks, after):
    height = S // 2 // chunks
    f32 = jnp.float32
    quarter = (QUARTERS, 2, S // QUARTERS, S)
    vmem = pl.BlockSpec(memory_space=pltpu.VMEM)
    return pl.pallas_call(
        slots_kernel,
        out_shape=(
            jax.ShapeDtypeStruct(quarter, f32),
            jax.ShapeDtypeStruct(quarter, f32),
            jax.ShapeDtypeStruct((2, *quarter), f32),
            jax.ShapeDtypeStruct((chunks, 5, height, S), f32),
            jax.ShapeDtypeStruct((chunks, 5, height, S), f32),
        ),
        in_specs=[
            pl.BlockSpec(memory_space=pltpu.SMEM), *[vmem] * 11, pl.BlockSpec(memory_space=pl.ANY)
        ],
        out_specs=[vmem] * 5,
        scratch_shapes=[
            pltpu.VMEM((2, 2 * S, 2 * S), f32),
            pltpu.VMEM((2, 2 * S, 2 * S), f32),
            pltpu.VMEM((5, S, S), f32),
        ],
        compiler_params=pltpu.CompilerParams(vmem_limit_bytes=54 * 1024 * 1024),
        name="slots",
    )(card, *blocks, probe, frames, *(jnp.asarray(t) for t in tables()), after)


def light_kernel(cards, probe, light, padded):
    power = jnp.zeros((S, S), jnp.float32)
    for m in range(2):
        power += probe[0, m] * probe[0, m] + probe[1, m] * probe[1, m]
    padded[...] = jnp.zeros_like(padded)
    padded[S : 2 * S, S : 2 * S] = power
    rows = S // QUARTERS
    first = S + lax.axis_index("pos") * rows
    sum_so_far = jnp.zeros((rows, S), jnp.float32)
    for post in range(QUARTERS):
        for tile in range(4):
            above, left = tile // 2, tile % 2

            def one_position(slot, sum_so_far):
                first_row = first + above * S - cards[post, tile, 2 * slot]
                first_column = S + left * S - cards[post, tile, 2 * slot + 1]
                inside, fine = lax.rem(first_row, 8), lax.rem(first_column, 128)
                block = padded[
                    pl.ds(pl.multiple_of(first_row - inside, 8), rows + 8),
                    pl.ds(pl.multiple_of(first_column - fine, 128), 384),
                ]
                return sum_so_far + cut(block, inside, fine)

            sum_so_far = lax.fori_loop(0, cards[post, tile, COUNT], one_position, sum_so_far)
    light[...] = sum_so_far


def run_light(cards, probe):
    vmem = pl.BlockSpec(memory_space=pltpu.VMEM)
    return pl.pallas_call(
        light_kernel,
        out_shape=jax.ShapeDtypeStruct((S // QUARTERS, S), jnp.float32),
        in_specs=[pl.BlockSpec(memory_space=pltpu.SMEM), vmem],
        out_specs=vmem,
        scratch_shapes=[pltpu.VMEM((3 * S + 8, 3 * S + 128), jnp.float32)],
        compiler_params=pltpu.CompilerParams(vmem_limit_bytes=54 * 1024 * 1024),
        name="light",
    )(cards, probe)


def moved(block, tiles_by, bands_by):
    tiles, bands = lax.axis_size(TILE), lax.axis_size("band")
    route = [
        (t * bands + b, (t + tiles_by) * bands + b + bands_by)
        for t in range(tiles)
        for b in range(bands)
        if t + tiles_by in range(tiles) and b + bands_by in range(bands)
    ]
    return lax.ppermute(block, (*TILE, "band"), route)


def across_cores(block):
    return lax.ppermute(block, "core", [(0, 1), (1, 0)])


def across_posts(block, bits):
    return lax.ppermute(block, "pos", [(p, p ^ bits) for p in range(QUARTERS)])


def exchanged(block, axes):
    return lax.all_to_all(block, axes, 0, 0)


def shared(block, axes):
    return exchanged(jnp.broadcast_to(block, (lax.axis_size(axes), *block.shape)), axes)


def corners(right, below):
    tiles, bands = lax.axis_size(TILE), lax.axis_size("band")
    across = [(t * bands + b, t * bands + b - 1) for t in range(1, tiles, 2) for b in range(1, bands)]
    return lax.ppermute(below, (*TILE, "band"), across), lax.ppermute(right, "core", [(1, 0)])


def on_device(object_planes, probe_planes, patterns, offsets, counts):
    core, band, post = (lax.axis_index(name) for name in ("core", "band", "pos"))
    bands, posts = lax.axis_size("band"), lax.axis_size("pos")
    plane = ("band", "pos")
    chunks = bands * posts
    right = moved(object_planes, 0, -1)
    below = moved(object_planes, -1, 0)
    card = jnp.pad(jnp.concatenate([offsets.reshape(6), counts.reshape(1)])[None], ((0, 0), (0, 121)))
    cards = [card, moved(card, 0, 1), moved(card, 1, 0), moved(card, 1, 1)]
    right, below, cards = lax.optimization_barrier((right, below, cards))
    corner_a, corner_b = corners(right, below)
    cards = shared(jnp.concatenate([*cards, jnp.zeros((4, 128), jnp.int32)]), "pos")
    top_left, top_right, bottom, keep, send = run_slots(
        card, (object_planes, right, below, corner_a, corner_b),
        probe_planes, patterns[0, 0, 0], chunks, cards,
    )

    from_above = moved(bottom, 1, 0)
    terms = keep + across_cores(send)
    terms = jnp.sum(exchanged(terms, plane), axis=0)
    terms, from_above = lax.optimization_barrier((terms, from_above))
    from_left = moved(top_right + from_above[1], 0, 1)
    terms = jnp.sum(shared(terms, "z_low"), axis=0)
    light = run_light(cards, probe_planes)
    terms, from_left, light = lax.optimization_barrier((terms, from_left, light))
    tile_sum = top_left + from_above[0] + from_left
    pieces = [lax.dynamic_index_in_dim(tile_sum, post ^ k, 0, keepdims=False) for k in range(QUARTERS)]
    pieces = [pieces[0], *(across_posts(pieces[k], k) for k in range(1, QUARTERS))]
    terms = jnp.sum(shared(terms, "z_high"), axis=0)

    rows = S // QUARTERS
    own_rows = lax.dynamic_slice_in_dim(object_planes, post * rows, rows, 1)
    own_rows = own_rows + sum(pieces[1:], pieces[0]) / (light + 1.0)
    object_new = jnp.zeros_like(object_planes)
    for k in range(QUARTERS):
        piece = across_posts(own_rows, k) if k else own_rows
        object_new = lax.dynamic_update_slice_in_dim(object_new, piece, (post ^ k) * rows, 1)

    height = S // 2 // chunks
    place = core * (S // 2) + (band * posts + post) * height
    own_probe = lax.dynamic_slice_in_dim(probe_planes.reshape(4, S, S), place, height, 1)
    own_probe = own_probe + terms[:4] / (terms[4] + 1.0)
    mine = shared(own_probe, plane).transpose(1, 0, 2, 3).reshape(4, S // 2, S)
    probe_new = jnp.zeros((4, S, S), jnp.float32)
    for half, at in ((mine, core), (across_cores(mine), 1 - core)):
        probe_new = lax.dynamic_update_slice_in_dim(probe_new, half, at * (S // 2), 1)
    return (object_new, probe_new.reshape(probe_planes.shape))


def solution(mesh):
    tiles, bands, posts = mesh.devices.shape
    low = min(4, tiles // 2)
    devices = mesh.devices.reshape(tiles // 2 // low, low, 2, bands, posts)
    mesh = jax.sharding.Mesh(devices, (*TILE, "band", "pos"))
    in_specs = (
        P(None, TILE, "band"),
        P(),
        P(TILE, "band", "pos", None, None, None),
        P(TILE, "band", "pos", None, None),
        P(TILE, "band", "pos"),
    )
    out_specs = (P(None, TILE, "band"), P())
    return jax.shard_map(
        on_device, mesh=mesh, in_specs=in_specs, out_specs=out_specs, check_vma=False
    )
```

```python
import functools
import math

import jax
import jax.numpy as jnp
import ml_dtypes
import numpy as np
from jax import lax
from jax.experimental import pallas as pl
from jax.experimental.pallas import tpu as pltpu
from jax.sharding import PartitionSpec as P

S = 256
QUARTERS = 4
COUNT = 6
TILE = ("z_high", "z_low", "core")


def tables():
    index = np.arange(S)
    angle = (index[:, None] * index[None, :] % S) * (2.0 * math.pi / S)
    cosine, sine = np.cos(angle) / 16.0, np.sin(angle) / 16.0
    left = np.block([[cosine, sine], [-sine, cosine]]).astype(np.float32)
    head = left.astype(ml_dtypes.bfloat16)
    rest = (left - head.astype(np.float32)).astype(ml_dtypes.bfloat16)
    return (head, rest, np.ascontiguousarray(head.T), np.ascontiguousarray(rest.T))


def split(value):
    head = value.astype(jnp.bfloat16)
    return head, (value - head.astype(jnp.float32)).astype(jnp.bfloat16)


def product(first, second):
    dot = functools.partial(jnp.dot, preferred_element_type=jnp.float32)
    return dot(first[0], second[0]) + dot(first[0], second[1]) + dot(first[1], second[0])


def regroup(value):
    return jnp.concatenate(
        [
            jnp.concatenate([value[:S, :S], value[S:, :S]], axis=1),
            jnp.concatenate([value[:S, S:], value[S:, S:]], axis=1),
        ],
        axis=0,
    )


def cut(block, row, column):
    height = block.shape[0]
    lane = lax.broadcasted_iota(jnp.int32, (height, 128), 1)
    turned = [pltpu.roll(block[:, k * 128 : k * 128 + 128], 128 - column, 1) for k in range(3)]
    block = jnp.concatenate(
        [jnp.where(lane < 128 - column, turned[k], turned[k + 1]) for k in range(2)], axis=1
    )
    turned = pltpu.roll(block.reshape(height // 8, 8, S), 8 - row, 1)
    within = lax.broadcasted_iota(jnp.int32, (height // 8 - 1, 8, S), 1)
    return jnp.where(within < 8 - row, turned[:-1], turned[1:]).reshape(height - 8, S)


def placed(value, row, column):
    turned = pltpu.roll(value.reshape(S // 8, 8, S), row, 1)
    gap = jnp.zeros((1, 8, S), jnp.float32)
    within = lax.broadcasted_iota(jnp.int32, (S // 8 + 1, 8, S), 1)
    value = jnp.where(
        within < row, jnp.concatenate([gap, turned], axis=0), jnp.concatenate([turned, gap], axis=0)
    ).reshape(S + 8, S)
    lane = lax.broadcasted_iota(jnp.int32, (S + 8, 128), 1)
    turned = [pltpu.roll(value[:, k * 128 : k * 128 + 128], column, 1) for k in range(2)]
    return jnp.concatenate(
        [
            jnp.where(lane < column, 0.0, turned[0]),
            jnp.where(lane < column, turned[0], turned[1]),
            jnp.where(lane < column, turned[1], 0.0),
        ],
        axis=1,
    )


def slots_kernel(
    card, own, right, below, corner_a, corner_b, probe, frames, lh, lr, rh, rr, after,
    top_left, top_right, bottom, keep, send, extended, total, terms,
):
    extended[:, :S, :S] = own[...]
    extended[:, :S, S:] = right[...]
    extended[:, S:, :S] = below[...]
    extended[:, S:, S:] = corner_a[...] + corner_b[...]
    total[...] = jnp.zeros_like(total)
    terms[...] = jnp.zeros_like(terms)
    blank = jnp.zeros((S, S), jnp.float32)

    def one_slot(slot, carry):
        row, column = card[0, 2 * slot], card[0, 2 * slot + 1]
        inside = lax.rem(row, 8)
        band_rows = pl.ds(pl.multiple_of(row - inside, 8), S + 8)
        fine = lax.rem(column, 128)
        band_columns = pl.ds(pl.multiple_of(column - fine, 128), 384)
        patch_real, patch_imag = (cut(extended[p, band_rows, band_columns], inside, fine) for p in range(2))
        left_table, right_table = (lh[...], lr[...]), (rh[...], rr[...])
        RC = 256
        wave = []
        for m in range(2):
            real = probe[0, m] * patch_real - probe[1, m] * patch_imag
            imag = probe[0, m] * patch_imag + probe[1, m] * patch_real
            wave.append(product(left_table, split(jnp.concatenate([real, imag], axis=0))))
        back = [[], []]
        for at in range(0, S, RC):
            part = slice(at, at + RC)
            far = [
                jnp.concatenate([wave[m][at : at + RC], wave[m][S + at : S + at + RC]], axis=1)
                for m in range(2)
            ]
            far = product(split(jnp.concatenate(far, axis=0)), right_table)
            power = far[:RC] * far[:RC] + far[RC:] * far[RC:]
            power = power[:, :S] + power[:, S:]
            change = jnp.sqrt(frames[slot, part]) / jnp.sqrt(power + 1.0) - 1.0
            change = jnp.concatenate([change, change], axis=0)
            swapped = jnp.concatenate([far[:, S:] * change, far[:, :S] * change], axis=1)
            chunk = product(split(swapped), right_table)
            for m in range(2):
                back[m].append(chunk[m * RC : m * RC + RC])
        object_real, object_imag = blank, blank
        for m in range(2):
            whole = jnp.concatenate([c[:, :S] for c in back[m]] + [c[:, S:] for c in back[m]], axis=0)
            chi = product(left_table, split(whole))
            chi_imag, chi_real = chi[:S], chi[S:]
            object_real += probe[0, m] * chi_real + probe[1, m] * chi_imag
            object_imag += probe[0, m] * chi_imag - probe[1, m] * chi_real
            terms[m] += patch_real * chi_real + patch_imag * chi_imag
            terms[2 + m] += patch_real * chi_imag - patch_imag * chi_real
        terms[4] += patch_real * patch_real + patch_imag * patch_imag
        for plane, value in enumerate((object_real, object_imag)):
            total[plane, band_rows, band_columns] += placed(value, inside, fine)
        return carry

    lax.fori_loop(0, card[0, COUNT], one_slot, 0)
    rows = S // QUARTERS
    for q in range(QUARTERS):
        upper, lower = slice(q * rows, (q + 1) * rows), slice(S + q * rows, S + (q + 1) * rows)
        top_left[q] = total[:, upper, :S]
        top_right[q] = total[:, upper, S:]
        bottom[0, q] = total[:, lower, :S]
        bottom[1, q] = total[:, lower, S:]
    chunks, _, height, _ = keep.shape
    core = lax.axis_index("core")
    for chunk in range(chunks):
        mine = pl.multiple_of(core * (S // 2) + chunk * height, height)
        other = pl.multiple_of((1 - core) * (S // 2) + chunk * height, height)
        for plane in range(5):
            keep[chunk, plane] = terms[plane, pl.ds(mine, height), :]
            send[chunk, plane] = terms[plane, pl.ds(other, height), :]


def run_slots(card, blocks, probe, frames, chunks, after):
    height = S // 2 // chunks
    f32 = jnp.float32
    quarter = (QUARTERS, 2, S // QUARTERS, S)
    vmem = pl.BlockSpec(memory_space=pltpu.VMEM)
    return pl.pallas_call(
        slots_kernel,
        out_shape=(
            jax.ShapeDtypeStruct(quarter, f32),
            jax.ShapeDtypeStruct(quarter, f32),
            jax.ShapeDtypeStruct((2, *quarter), f32),
            jax.ShapeDtypeStruct((chunks, 5, height, S), f32),
            jax.ShapeDtypeStruct((chunks, 5, height, S), f32),
        ),
        in_specs=[
            pl.BlockSpec(memory_space=pltpu.SMEM), *[vmem] * 11, pl.BlockSpec(memory_space=pl.ANY)
        ],
        out_specs=[vmem] * 5,
        scratch_shapes=[
            pltpu.VMEM((2, 2 * S, 2 * S), f32),
            pltpu.VMEM((2, 2 * S, 2 * S), f32),
            pltpu.VMEM((5, S, S), f32),
        ],
        compiler_params=pltpu.CompilerParams(vmem_limit_bytes=54 * 1024 * 1024),
        name="slots",
    )(card, *blocks, probe, frames, *(jnp.asarray(t) for t in tables()), after)


def light_kernel(card, probe, top_left, top_right, bottom, total):
    power = jnp.zeros((S, S), jnp.float32)
    for m in range(2):
        power += probe[0, m] * probe[0, m] + probe[1, m] * probe[1, m]
    total[...] = jnp.zeros_like(total)

    def one_slot(slot, carry):
        row, column = card[0, 2 * slot], card[0, 2 * slot + 1]
        inside, fine = lax.rem(row, 8), lax.rem(column, 128)
        band_rows = pl.ds(pl.multiple_of(row - inside, 8), S + 8)
        band_columns = pl.ds(pl.multiple_of(column - fine, 128), 384)
        total[band_rows, band_columns] += placed(power, inside, fine)
        return carry

    lax.fori_loop(0, card[0, COUNT], one_slot, 0)
    top_left[...] = total[:S, :S]
    top_right[...] = total[:S, S:]
    bottom[0] = total[S:, :S]
    bottom[1] = total[S:, S:]


def run_light(card, probe):
    vmem = pl.BlockSpec(memory_space=pltpu.VMEM)
    tile = jax.ShapeDtypeStruct((S, S), jnp.float32)
    return pl.pallas_call(
        light_kernel,
        out_shape=(tile, tile, jax.ShapeDtypeStruct((2, S, S), jnp.float32)),
        in_specs=[pl.BlockSpec(memory_space=pltpu.SMEM), vmem],
        out_specs=[vmem] * 3,
        scratch_shapes=[pltpu.VMEM((2 * S, 2 * S), jnp.float32)],
        compiler_params=pltpu.CompilerParams(vmem_limit_bytes=54 * 1024 * 1024),
        name="light",
    )(card, probe)


def moved(block, tiles_by, bands_by):
    tiles, bands = lax.axis_size(TILE), lax.axis_size("band")
    route = [
        (t * bands + b, (t + tiles_by) * bands + b + bands_by)
        for t in range(tiles)
        for b in range(bands)
        if t + tiles_by in range(tiles) and b + bands_by in range(bands)
    ]
    return lax.ppermute(block, (*TILE, "band"), route)


def across_cores(block):
    return lax.ppermute(block, "core", [(0, 1), (1, 0)])


def across_posts(block, bits):
    return lax.ppermute(block, "pos", [(p, p ^ bits) for p in range(QUARTERS)])


def exchanged(block, axes):
    return lax.all_to_all(block, axes, 0, 0)


def shared(block, axes):
    return exchanged(jnp.broadcast_to(block, (lax.axis_size(axes), *block.shape)), axes)


def corners(right, below):
    tiles, bands = lax.axis_size(TILE), lax.axis_size("band")
    across = [(t * bands + b, t * bands + b - 1) for t in range(1, tiles, 2) for b in range(1, bands)]
    return lax.ppermute(below, (*TILE, "band"), across), lax.ppermute(right, "core", [(1, 0)])


def on_device(object_planes, probe_planes, patterns, offsets, counts):
    core, band, post = (lax.axis_index(name) for name in ("core", "band", "pos"))
    bands, posts = lax.axis_size("band"), lax.axis_size("pos")
    plane = ("band", "pos")
    chunks = bands * posts
    right = moved(object_planes, 0, -1)
    below = moved(object_planes, -1, 0)
    card = jnp.pad(jnp.concatenate([offsets.reshape(6), counts.reshape(1)])[None], ((0, 0), (0, 121)))
    light, light_right, light_bottom = run_light(card, probe_planes)
    right, below, light_bottom = lax.optimization_barrier((right, below, light_bottom))
    light_above = moved(light_bottom, 1, 0)
    corner_a, corner_b = corners(right, below)
    light_left = moved(light_right + light_above[1], 0, 1)
    light = light + light_above[0]
    top_left, top_right, bottom, keep, send = run_slots(
        card, (object_planes, right, below, corner_a, corner_b),
        probe_planes, patterns[0, 0, 0], chunks, light_above,
    )

    light = lax.psum_scatter(light + light_left, "pos", scatter_dimension=0, tiled=True)
    from_above = moved(bottom, 1, 0)
    terms = keep + across_cores(send)
    terms = jnp.sum(exchanged(terms, plane), axis=0)
    terms, from_above = lax.optimization_barrier((terms, from_above))
    from_left = moved(top_right + from_above[1], 0, 1)
    terms = jnp.sum(shared(terms, "z_low"), axis=0)
    tile_sum = top_left + from_above[0] + from_left
    tile_sum = lax.psum_scatter(tile_sum, "pos", scatter_dimension=0, tiled=True)[0]
    terms = jnp.sum(shared(terms, "z_high"), axis=0)

    rows = S // QUARTERS
    own_rows = lax.dynamic_slice_in_dim(object_planes, post * rows, rows, 1)
    own_rows = own_rows + tile_sum / (light + 1.0)
    object_new = jnp.zeros_like(object_planes)
    for k in range(QUARTERS):
        piece = across_posts(own_rows, k) if k else own_rows
        object_new = lax.dynamic_update_slice_in_dim(object_new, piece, (post ^ k) * rows, 1)

    height = S // 2 // chunks
    place = core * (S // 2) + (band * posts + post) * height
    own_probe = lax.dynamic_slice_in_dim(probe_planes.reshape(4, S, S), place, height, 1)
    own_probe = own_probe + terms[:4] / (terms[4] + 1.0)
    mine = shared(own_probe, plane).transpose(1, 0, 2, 3).reshape(4, S // 2, S)
    probe_new = jnp.zeros((4, S, S), jnp.float32)
    for half, at in ((mine, core), (across_cores(mine), 1 - core)):
        probe_new = lax.dynamic_update_slice_in_dim(probe_new, half, at * (S // 2), 1)
    return (object_new, probe_new.reshape(probe_planes.shape))


def solution(mesh):
    tiles, bands, posts = mesh.devices.shape
    low = min(4, tiles // 2)
    devices = mesh.devices.reshape(tiles // 2 // low, low, 2, bands, posts)
    mesh = jax.sharding.Mesh(devices, (*TILE, "band", "pos"))
    in_specs = (
        P(None, TILE, "band"),
        P(),
        P(TILE, "band", "pos", None, None, None),
        P(TILE, "band", "pos", None, None),
        P(TILE, "band", "pos"),
    )
    out_specs = (P(None, TILE, "band"), P())
    return jax.shard_map(
        on_device, mesh=mesh, in_specs=in_specs, out_specs=out_specs, check_vma=False
    )
```

```python
import functools
import math

import jax
import jax.numpy as jnp
import ml_dtypes
import numpy as np
from jax import lax
from jax.experimental import pallas as pl
from jax.experimental.pallas import tpu as pltpu
from jax.sharding import PartitionSpec as P

S = 256
COUNT = 6
TILE = ("z_high", "z_low", "core")


def tables():
    index = np.arange(S)
    angle = (index[:, None] * index[None, :] % S) * (2.0 * math.pi / S)
    cosine, sine = np.cos(angle) / 16.0, np.sin(angle) / 16.0
    left = np.block([[cosine, sine], [-sine, cosine]]).astype(np.float32)
    head = left.astype(ml_dtypes.bfloat16)
    rest = (left - head.astype(np.float32)).astype(ml_dtypes.bfloat16)
    return (head, rest, np.ascontiguousarray(head.T), np.ascontiguousarray(rest.T))


def split(value):
    head = value.astype(jnp.bfloat16)
    return head, (value - head.astype(jnp.float32)).astype(jnp.bfloat16)


def product(first, second):
    dot = functools.partial(jnp.dot, preferred_element_type=jnp.float32)
    return dot(first[0], second[0]) + dot(first[0], second[1]) + dot(first[1], second[0])


def regroup(value):
    return jnp.concatenate(
        [
            jnp.concatenate([value[:S, :S], value[S:, :S]], axis=1),
            jnp.concatenate([value[:S, S:], value[S:, S:]], axis=1),
        ],
        axis=0,
    )


def cut(block, row, column):
    height = block.shape[0]
    lane = lax.broadcasted_iota(jnp.int32, (height, 128), 1)
    turned = [pltpu.roll(block[:, k * 128 : k * 128 + 128], 128 - column, 1) for k in range(3)]
    block = jnp.concatenate(
        [jnp.where(lane < 128 - column, turned[k], turned[k + 1]) for k in range(2)], axis=1
    )
    turned = pltpu.roll(block.reshape(height // 8, 8, S), 8 - row, 1)
    within = lax.broadcasted_iota(jnp.int32, (height // 8 - 1, 8, S), 1)
    return jnp.where(within < 8 - row, turned[:-1], turned[1:]).reshape(height - 8, S)


def placed(value, row, column):
    turned = pltpu.roll(value.reshape(S // 8, 8, S), row, 1)
    gap = jnp.zeros((1, 8, S), jnp.float32)
    within = lax.broadcasted_iota(jnp.int32, (S // 8 + 1, 8, S), 1)
    value = jnp.where(
        within < row, jnp.concatenate([gap, turned], axis=0), jnp.concatenate([turned, gap], axis=0)
    ).reshape(S + 8, S)
    lane = lax.broadcasted_iota(jnp.int32, (S + 8, 128), 1)
    turned = [pltpu.roll(value[:, k * 128 : k * 128 + 128], column, 1) for k in range(2)]
    return jnp.concatenate(
        [
            jnp.where(lane < column, 0.0, turned[0]),
            jnp.where(lane < column, turned[0], turned[1]),
            jnp.where(lane < column, turned[1], 0.0),
        ],
        axis=1,
    )


def slots_kernel(
    card, own, right, below, corner_a, corner_b, probe, frames, lh, lr, rh, rr, after,
    top_left, top_right, bottom, keep, send, extended, total, terms,
):
    extended[:, :S, :S] = own[...]
    extended[:, :S, S:] = right[...]
    extended[:, S:, :S] = below[...]
    extended[:, S:, S:] = corner_a[...] + corner_b[...]
    total[...] = jnp.zeros_like(total)
    terms[...] = jnp.zeros_like(terms)
    blank = jnp.zeros((S, S), jnp.float32)

    def one_slot(slot, carry):
        row, column = card[0, 2 * slot], card[0, 2 * slot + 1]
        inside = lax.rem(row, 8)
        band_rows = pl.ds(pl.multiple_of(row - inside, 8), S + 8)
        fine = lax.rem(column, 128)
        band_columns = pl.ds(pl.multiple_of(column - fine, 128), 384)
        patch_real, patch_imag = (cut(extended[p, band_rows, band_columns], inside, fine) for p in range(2))
        left_table, right_table = (lh[...], lr[...]), (rh[...], rr[...])
        RC = 256
        wave = []
        for m in range(2):
            real = probe[0, m] * patch_real - probe[1, m] * patch_imag
            imag = probe[0, m] * patch_imag + probe[1, m] * patch_real
            wave.append(product(left_table, split(jnp.concatenate([real, imag], axis=0))))
        back = [[], []]
        for at in range(0, S, RC):
            part = slice(at, at + RC)
            far = [
                jnp.concatenate([wave[m][at : at + RC], wave[m][S + at : S + at + RC]], axis=1)
                for m in range(2)
            ]
            far = product(split(jnp.concatenate(far, axis=0)), right_table)
            power = far[:RC] * far[:RC] + far[RC:] * far[RC:]
            power = power[:, :S] + power[:, S:]
            change = jnp.sqrt(frames[slot, part]) / jnp.sqrt(power + 1.0) - 1.0
            change = jnp.concatenate([change, change], axis=0)
            swapped = jnp.concatenate([far[:, S:] * change, far[:, :S] * change], axis=1)
            chunk = product(split(swapped), right_table)
            for m in range(2):
                back[m].append(chunk[m * RC : m * RC + RC])
        object_real, object_imag = blank, blank
        for m in range(2):
            whole = jnp.concatenate([c[:, :S] for c in back[m]] + [c[:, S:] for c in back[m]], axis=0)
            chi = product(left_table, split(whole))
            chi_imag, chi_real = chi[:S], chi[S:]
            object_real += probe[0, m] * chi_real + probe[1, m] * chi_imag
            object_imag += probe[0, m] * chi_imag - probe[1, m] * chi_real
            terms[m] += patch_real * chi_real + patch_imag * chi_imag
            terms[2 + m] += patch_real * chi_imag - patch_imag * chi_real
        terms[4] += patch_real * patch_real + patch_imag * patch_imag
        for plane, value in enumerate((object_real, object_imag)):
            total[plane, band_rows, band_columns] += placed(value, inside, fine)
        return carry

    lax.fori_loop(0, card[0, COUNT], one_slot, 0)
    top_left[...] = total[:, :S, :S]
    top_right[...] = total[:, :S, S:]
    bottom[0] = total[:, S:, :S]
    bottom[1] = total[:, S:, S:]
    chunks, _, height, _ = keep.shape
    core = lax.axis_index("core")
    for chunk in range(chunks):
        mine = pl.multiple_of(core * (S // 2) + chunk * height, height)
        other = pl.multiple_of((1 - core) * (S // 2) + chunk * height, height)
        for plane in range(5):
            keep[chunk, plane] = terms[plane, pl.ds(mine, height), :]
            send[chunk, plane] = terms[plane, pl.ds(other, height), :]


def run_slots(card, blocks, probe, frames, chunks, after):
    height = S // 2 // chunks
    f32 = jnp.float32
    tile = (2, S, S)
    vmem = pl.BlockSpec(memory_space=pltpu.VMEM)
    return pl.pallas_call(
        slots_kernel,
        out_shape=(
            jax.ShapeDtypeStruct(tile, f32),
            jax.ShapeDtypeStruct(tile, f32),
            jax.ShapeDtypeStruct((2, *tile), f32),
            jax.ShapeDtypeStruct((chunks, 5, height, S), f32),
            jax.ShapeDtypeStruct((chunks, 5, height, S), f32),
        ),
        in_specs=[
            pl.BlockSpec(memory_space=pltpu.SMEM), *[vmem] * 11, pl.BlockSpec(memory_space=pl.ANY)
        ],
        out_specs=[vmem] * 5,
        scratch_shapes=[
            pltpu.VMEM((2, 2 * S, 2 * S), f32),
            pltpu.VMEM((2, 2 * S, 2 * S), f32),
            pltpu.VMEM((5, S, S), f32),
        ],
        compiler_params=pltpu.CompilerParams(vmem_limit_bytes=54 * 1024 * 1024),
        name="slots",
    )(card, *blocks, probe, frames, *(jnp.asarray(t) for t in tables()), after)


def light_kernel(card, probe, top_left, top_right, bottom, total):
    power = jnp.zeros((S, S), jnp.float32)
    for m in range(2):
        power += probe[0, m] * probe[0, m] + probe[1, m] * probe[1, m]
    total[...] = jnp.zeros_like(total)

    def one_slot(slot, carry):
        row, column = card[0, 2 * slot], card[0, 2 * slot + 1]
        inside, fine = lax.rem(row, 8), lax.rem(column, 128)
        band_rows = pl.ds(pl.multiple_of(row - inside, 8), S + 8)
        band_columns = pl.ds(pl.multiple_of(column - fine, 128), 384)
        total[band_rows, band_columns] += placed(power, inside, fine)
        return carry

    lax.fori_loop(0, card[0, COUNT], one_slot, 0)
    top_left[...] = total[:S, :S]
    top_right[...] = total[:S, S:]
    bottom[0] = total[S:, :S]
    bottom[1] = total[S:, S:]


def run_light(card, probe):
    vmem = pl.BlockSpec(memory_space=pltpu.VMEM)
    tile = jax.ShapeDtypeStruct((S, S), jnp.float32)
    return pl.pallas_call(
        light_kernel,
        out_shape=(tile, tile, jax.ShapeDtypeStruct((2, S, S), jnp.float32)),
        in_specs=[pl.BlockSpec(memory_space=pltpu.SMEM), vmem],
        out_specs=[vmem] * 3,
        scratch_shapes=[pltpu.VMEM((2 * S, 2 * S), jnp.float32)],
        compiler_params=pltpu.CompilerParams(vmem_limit_bytes=54 * 1024 * 1024),
        name="light",
    )(card, probe)


def moved(block, tiles_by, bands_by):
    tiles, bands = lax.axis_size(TILE), lax.axis_size("band")
    route = [
        (t * bands + b, (t + tiles_by) * bands + b + bands_by)
        for t in range(tiles)
        for b in range(bands)
        if t + tiles_by in range(tiles) and b + bands_by in range(bands)
    ]
    return lax.ppermute(block, (*TILE, "band"), route)


def across_cores(block):
    return lax.ppermute(block, "core", [(0, 1), (1, 0)])


def sum_over_posts(block):
    for bits in (1, 3):
        block = block + lax.ppermute(block, "pos", [(p, p ^ bits) for p in range(4)])
    return block


def exchanged(block, axes):
    return lax.all_to_all(block, axes, 0, 0)


def shared(block, axes):
    return exchanged(jnp.broadcast_to(block, (lax.axis_size(axes), *block.shape)), axes)


def corners(right, below):
    tiles, bands = lax.axis_size(TILE), lax.axis_size("band")
    across = [(t * bands + b, t * bands + b - 1) for t in range(1, tiles, 2) for b in range(1, bands)]
    return lax.ppermute(below, (*TILE, "band"), across), lax.ppermute(right, "core", [(1, 0)])


def on_device(object_planes, probe_planes, patterns, offsets, counts):
    core, band, post = (lax.axis_index(name) for name in ("core", "band", "pos"))
    bands, posts = lax.axis_size("band"), lax.axis_size("pos")
    plane = ("band", "pos")
    chunks = bands * posts
    right = moved(object_planes, 0, -1)
    below = moved(object_planes, -1, 0)
    card = jnp.pad(jnp.concatenate([offsets.reshape(6), counts.reshape(1)])[None], ((0, 0), (0, 121)))
    light, light_right, light_bottom = run_light(card, probe_planes)
    right, below, light_bottom = lax.optimization_barrier((right, below, light_bottom))
    light_above = moved(light_bottom, 1, 0)
    corner_a, corner_b = corners(right, below)
    light_left = moved(light_right + light_above[1], 0, 1)
    light = light + light_above[0]
    top_left, top_right, bottom, keep, send = run_slots(
        card, (object_planes, right, below, corner_a, corner_b),
        probe_planes, patterns[0, 0, 0], chunks, light_above,
    )

    light = sum_over_posts(light + light_left)
    from_above = moved(bottom, 1, 0)
    terms = keep + across_cores(send)
    terms = jnp.sum(exchanged(terms, plane), axis=0)
    terms, right_sum = lax.optimization_barrier((terms, top_right + from_above[1]))
    from_left = moved(right_sum, 0, 1)
    terms = jnp.sum(shared(terms, "z_low"), axis=0)
    tile_sum = top_left + from_above[0] + from_left
    tile_sum = sum_over_posts(tile_sum)
    object_new = object_planes + tile_sum / (light + 1.0)
    terms = jnp.sum(shared(terms, "z_high"), axis=0)

    height = S // 2 // chunks
    place = core * (S // 2) + (band * posts + post) * height
    own_probe = lax.dynamic_slice_in_dim(probe_planes.reshape(4, S, S), place, height, 1)
    own_probe = own_probe + terms[:4] / (terms[4] + 1.0)
    mine = shared(own_probe, plane).transpose(1, 0, 2, 3).reshape(4, S // 2, S)
    probe_new = jnp.zeros((4, S, S), jnp.float32)
    for half, at in ((mine, core), (across_cores(mine), 1 - core)):
        probe_new = lax.dynamic_update_slice_in_dim(probe_new, half, at * (S // 2), 1)
    return (object_new, probe_new.reshape(probe_planes.shape))


def solution(mesh):
    tiles, bands, posts = mesh.devices.shape
    low = min(4, tiles // 2)
    devices = mesh.devices.reshape(tiles // 2 // low, low, 2, bands, posts)
    mesh = jax.sharding.Mesh(devices, (*TILE, "band", "pos"))
    in_specs = (
        P(None, TILE, "band"),
        P(),
        P(TILE, "band", "pos", None, None, None),
        P(TILE, "band", "pos", None, None),
        P(TILE, "band", "pos"),
    )
    out_specs = (P(None, TILE, "band"), P())
    return jax.shard_map(
        on_device, mesh=mesh, in_specs=in_specs, out_specs=out_specs, check_vma=False
    )
```

```python
import functools
import math

import jax
import jax.numpy as jnp
import ml_dtypes
import numpy as np
from jax import lax
from jax.experimental import pallas as pl
from jax.experimental.pallas import tpu as pltpu
from jax.sharding import PartitionSpec as P

S = 256
COUNT = 6
TILE = ("z_high", "z_low", "core")


def tables():
    index = np.arange(S)
    angle = (index[:, None] * index[None, :] % S) * (2.0 * math.pi / S)
    cosine, sine = np.cos(angle) / 16.0, np.sin(angle) / 16.0
    left = np.block([[cosine, sine], [-sine, cosine]]).astype(np.float32)
    head = left.astype(ml_dtypes.bfloat16)
    rest = (left - head.astype(np.float32)).astype(ml_dtypes.bfloat16)
    return (head, rest, np.ascontiguousarray(head.T), np.ascontiguousarray(rest.T))


def split(value):
    head = value.astype(jnp.bfloat16)
    return head, (value - head.astype(jnp.float32)).astype(jnp.bfloat16)


def product(first, second):
    dot = functools.partial(jnp.dot, preferred_element_type=jnp.float32)
    return dot(first[0], second[0]) + dot(first[0], second[1]) + dot(first[1], second[0])


def regroup(value):
    return jnp.concatenate(
        [
            jnp.concatenate([value[:S, :S], value[S:, :S]], axis=1),
            jnp.concatenate([value[:S, S:], value[S:, S:]], axis=1),
        ],
        axis=0,
    )


def cut(block, row, column):
    height = block.shape[0]
    lane = lax.broadcasted_iota(jnp.int32, (height, 128), 1)
    turned = [pltpu.roll(block[:, k * 128 : k * 128 + 128], 128 - column, 1) for k in range(3)]
    block = jnp.concatenate(
        [jnp.where(lane < 128 - column, turned[k], turned[k + 1]) for k in range(2)], axis=1
    )
    turned = pltpu.roll(block.reshape(height // 8, 8, S), 8 - row, 1)
    within = lax.broadcasted_iota(jnp.int32, (height // 8 - 1, 8, S), 1)
    return jnp.where(within < 8 - row, turned[:-1], turned[1:]).reshape(height - 8, S)


def placed(value, row, column):
    turned = pltpu.roll(value.reshape(S // 8, 8, S), row, 1)
    gap = jnp.zeros((1, 8, S), jnp.float32)
    within = lax.broadcasted_iota(jnp.int32, (S // 8 + 1, 8, S), 1)
    value = jnp.where(
        within < row, jnp.concatenate([gap, turned], axis=0), jnp.concatenate([turned, gap], axis=0)
    ).reshape(S + 8, S)
    lane = lax.broadcasted_iota(jnp.int32, (S + 8, 128), 1)
    turned = [pltpu.roll(value[:, k * 128 : k * 128 + 128], column, 1) for k in range(2)]
    return jnp.concatenate(
        [
            jnp.where(lane < column, 0.0, turned[0]),
            jnp.where(lane < column, turned[0], turned[1]),
            jnp.where(lane < column, turned[1], 0.0),
        ],
        axis=1,
    )


def slots_kernel(
    card, own, right, below, corner_a, corner_b, probe, frames, lh, lr, rh, rr, after,
    top_left, top_right, bottom, keep, send, extended, total, terms,
):
    extended[:, :S, :S] = own[...]
    extended[:, :S, S:] = right[...]
    extended[:, S:, :S] = below[...]
    extended[:, S:, S:] = corner_a[...] + corner_b[...]
    total[...] = jnp.zeros_like(total)
    terms[...] = jnp.zeros_like(terms)
    blank = jnp.zeros((S, S), jnp.float32)

    def one_slot(slot, carry):
        row, column = card[0, 2 * slot], card[0, 2 * slot + 1]
        inside = lax.rem(row, 8)
        band_rows = pl.ds(pl.multiple_of(row - inside, 8), S + 8)
        fine = lax.rem(column, 128)
        band_columns = pl.ds(pl.multiple_of(column - fine, 128), 384)
        patch_real, patch_imag = (cut(extended[p, band_rows, band_columns], inside, fine) for p in range(2))
        left_table, right_table = (lh[...], lr[...]), (rh[...], rr[...])
        RC = 256
        wave = []
        for m in range(2):
            real = probe[0, m] * patch_real - probe[1, m] * patch_imag
            imag = probe[0, m] * patch_imag + probe[1, m] * patch_real
            wave.append(product(left_table, split(jnp.concatenate([real, imag], axis=0))))
        back = [[], []]
        for at in range(0, S, RC):
            part = slice(at, at + RC)
            far = [
                jnp.concatenate([wave[m][at : at + RC], wave[m][S + at : S + at + RC]], axis=1)
                for m in range(2)
            ]
            far = product(split(jnp.concatenate(far, axis=0)), right_table)
            power = far[:RC] * far[:RC] + far[RC:] * far[RC:]
            power = power[:, :S] + power[:, S:]
            change = jnp.sqrt(frames[slot, part]) / jnp.sqrt(power + 1.0) - 1.0
            change = jnp.concatenate([change, change], axis=0)
            swapped = jnp.concatenate([far[:, S:] * change, far[:, :S] * change], axis=1)
            chunk = product(split(swapped), right_table)
            for m in range(2):
                back[m].append(chunk[m * RC : m * RC + RC])
        object_real, object_imag = blank, blank
        for m in range(2):
            whole = jnp.concatenate([c[:, :S] for c in back[m]] + [c[:, S:] for c in back[m]], axis=0)
            chi = product(left_table, split(whole))
            chi_imag, chi_real = chi[:S], chi[S:]
            object_real += probe[0, m] * chi_real + probe[1, m] * chi_imag
            object_imag += probe[0, m] * chi_imag - probe[1, m] * chi_real
            terms[m] += patch_real * chi_real + patch_imag * chi_imag
            terms[2 + m] += patch_real * chi_imag - patch_imag * chi_real
        terms[4] += patch_real * patch_real + patch_imag * patch_imag
        for plane, value in enumerate((object_real, object_imag)):
            total[plane, band_rows, band_columns] += placed(value, inside, fine)
        return carry

    lax.fori_loop(0, card[0, COUNT], one_slot, 0)
    top_left[...] = total[:, :S, :S]
    top_right[...] = total[:, :S, S:]
    bottom[0] = total[:, S:, :S]
    bottom[1] = total[:, S:, S:]
    chunks, _, height, _ = keep.shape
    core = lax.axis_index("core")
    for chunk in range(chunks):
        mine = pl.multiple_of(core * (S // 2) + chunk * height, height)
        other = pl.multiple_of((1 - core) * (S // 2) + chunk * height, height)
        for plane in range(5):
            keep[chunk, plane] = terms[plane, pl.ds(mine, height), :]
            send[chunk, plane] = terms[plane, pl.ds(other, height), :]


def run_slots(card, blocks, probe, frames, chunks, after):
    height = S // 2 // chunks
    f32 = jnp.float32
    tile = (2, S, S)
    vmem = pl.BlockSpec(memory_space=pltpu.VMEM)
    return pl.pallas_call(
        slots_kernel,
        out_shape=(
            jax.ShapeDtypeStruct(tile, f32),
            jax.ShapeDtypeStruct(tile, f32),
            jax.ShapeDtypeStruct((2, *tile), f32),
            jax.ShapeDtypeStruct((chunks, 5, height, S), f32),
            jax.ShapeDtypeStruct((chunks, 5, height, S), f32),
        ),
        in_specs=[
            pl.BlockSpec(memory_space=pltpu.SMEM), *[vmem] * 11, pl.BlockSpec(memory_space=pl.ANY)
        ],
        out_specs=[vmem] * 5,
        scratch_shapes=[
            pltpu.VMEM((2, 2 * S, 2 * S), f32),
            pltpu.VMEM((2, 2 * S, 2 * S), f32),
            pltpu.VMEM((5, S, S), f32),
        ],
        compiler_params=pltpu.CompilerParams(vmem_limit_bytes=54 * 1024 * 1024),
        name="slots",
    )(card, *blocks, probe, frames, *(jnp.asarray(t) for t in tables()), after)


def light_kernel(cards, probe, own, right, below, corner, total):
    power = jnp.zeros((S, S), jnp.float32)
    for m in range(2):
        power += probe[0, m] * probe[0, m] + probe[1, m] * probe[1, m]
    total[...] = jnp.zeros_like(total)

    for post in range(cards.shape[0]):

        def one_slot(slot, carry):
            row, column = cards[post, 0, 2 * slot], cards[post, 0, 2 * slot + 1]
            inside, fine = lax.rem(row, 8), lax.rem(column, 128)
            band_rows = pl.ds(pl.multiple_of(row - inside, 8), S + 8)
            band_columns = pl.ds(pl.multiple_of(column - fine, 128), 384)
            total[band_rows, band_columns] += placed(power, inside, fine)
            return carry

        lax.fori_loop(0, cards[post, 0, COUNT], one_slot, 0)
    own[...] = total[:S, :S]
    right[...] = total[:S, S:]
    below[...] = total[S:, :S]
    corner[...] = total[S:, S:]


def run_light(cards, probe):
    vmem = pl.BlockSpec(memory_space=pltpu.VMEM)
    return pl.pallas_call(
        light_kernel,
        out_shape=(jax.ShapeDtypeStruct((S, S), jnp.float32),) * 4,
        in_specs=[pl.BlockSpec(memory_space=pltpu.SMEM), vmem],
        out_specs=[vmem] * 4,
        scratch_shapes=[pltpu.VMEM((2 * S, 2 * S), jnp.float32)],
        compiler_params=pltpu.CompilerParams(vmem_limit_bytes=54 * 1024 * 1024),
        name="light",
    )(cards, probe)


def moved(block, tiles_by, bands_by):
    tiles, bands = lax.axis_size(TILE), lax.axis_size("band")
    route = [
        (t * bands + b, (t + tiles_by) * bands + b + bands_by)
        for t in range(tiles)
        for b in range(bands)
        if t + tiles_by in range(tiles) and b + bands_by in range(bands)
    ]
    return lax.ppermute(block, (*TILE, "band"), route)


def across_cores(block):
    return lax.ppermute(block, "core", [(0, 1), (1, 0)])


def sum_over_posts(block):
    for bits in (1, 3):
        block = block + lax.ppermute(block, "pos", [(p, p ^ bits) for p in range(4)])
    return block


def exchanged(block, axes):
    return lax.all_to_all(block, axes, 0, 0)


def shared(block, axes):
    return exchanged(jnp.broadcast_to(block, (lax.axis_size(axes), *block.shape)), axes)


def corners(right, below):
    tiles, bands = lax.axis_size(TILE), lax.axis_size("band")
    across = [(t * bands + b, t * bands + b - 1) for t in range(1, tiles, 2) for b in range(1, bands)]
    return lax.ppermute(below, (*TILE, "band"), across), lax.ppermute(right, "core", [(1, 0)])


def on_device(object_planes, probe_planes, patterns, offsets, counts):
    core, band, post = (lax.axis_index(name) for name in ("core", "band", "pos"))
    bands, posts = lax.axis_size("band"), lax.axis_size("pos")
    plane = ("band", "pos")
    chunks = bands * posts
    right = moved(object_planes, 0, -1)
    below = moved(object_planes, -1, 0)
    card = jnp.pad(jnp.concatenate([offsets.reshape(6), counts.reshape(1)])[None], ((0, 0), (0, 121)))
    light, *spill = run_light(shared(card, "pos"), probe_planes)
    right, below, spill = lax.optimization_barrier((right, below, spill))
    corner_a, corner_b = corners(right, below)
    light = light + moved(spill[0], 0, 1) + moved(spill[1], 1, 0) + moved(spill[2], 1, 1)
    top_left, top_right, bottom, keep, send = run_slots(
        card, (object_planes, right, below, corner_a, corner_b),
        probe_planes, patterns[0, 0, 0], chunks, light,
    )

    from_above = moved(bottom, 1, 0)
    terms = keep + across_cores(send)
    terms = jnp.sum(exchanged(terms, plane), axis=0)
    terms, from_above = lax.optimization_barrier((terms, from_above))
    from_left = moved(top_right + from_above[1], 0, 1)
    terms = jnp.sum(shared(terms, "z_high"), axis=0)
    terms, from_left = lax.optimization_barrier((terms, from_left))
    tile_sum = top_left + from_above[0] + from_left
    tile_sum = sum_over_posts(tile_sum)
    object_new = object_planes + tile_sum / (light + 1.0)
    terms = jnp.sum(shared(terms, "z_low"), axis=0)

    height = S // 2 // chunks
    place = core * (S // 2) + (band * posts + post) * height
    own_probe = lax.dynamic_slice_in_dim(probe_planes.reshape(4, S, S), place, height, 1)
    own_probe = own_probe + terms[:4] / (terms[4] + 1.0)
    mine = shared(own_probe, plane).transpose(1, 0, 2, 3).reshape(4, S // 2, S)
    probe_new = jnp.zeros((4, S, S), jnp.float32)
    for half, at in ((mine, core), (across_cores(mine), 1 - core)):
        probe_new = lax.dynamic_update_slice_in_dim(probe_new, half, at * (S // 2), 1)
    return (object_new, probe_new.reshape(probe_planes.shape))


def solution(mesh):
    tiles, bands, posts = mesh.devices.shape
    low = min(4, tiles // 2)
    devices = mesh.devices.reshape(tiles // 2 // low, low, 2, bands, posts)
    mesh = jax.sharding.Mesh(devices, (*TILE, "band", "pos"))
    in_specs = (
        P(None, TILE, "band"),
        P(),
        P(TILE, "band", "pos", None, None, None),
        P(TILE, "band", "pos", None, None),
        P(TILE, "band", "pos"),
    )
    out_specs = (P(None, TILE, "band"), P())
    return jax.shard_map(
        on_device, mesh=mesh, in_specs=in_specs, out_specs=out_specs, check_vma=False
    )
```

```python
import functools
import math

import jax
import jax.numpy as jnp
import ml_dtypes
import numpy as np
from jax import lax
from jax.experimental import pallas as pl
from jax.experimental.pallas import tpu as pltpu
from jax.sharding import PartitionSpec as P

S = 256
QUARTERS = 4
COUNT = 6
TILE = ("z_high", "z_low", "core")


def tables():
    index = np.arange(S)
    angle = (index[:, None] * index[None, :] % S) * (2.0 * math.pi / S)
    cosine, sine = np.cos(angle) / 16.0, np.sin(angle) / 16.0
    left = np.block([[cosine, sine], [-sine, cosine]]).astype(np.float32)
    head = left.astype(ml_dtypes.bfloat16)
    rest = (left - head.astype(np.float32)).astype(ml_dtypes.bfloat16)
    return (head, rest, np.ascontiguousarray(head.T), np.ascontiguousarray(rest.T))


def split(value):
    head = value.astype(jnp.bfloat16)
    return head, (value - head.astype(jnp.float32)).astype(jnp.bfloat16)


def product(first, second):
    dot = functools.partial(jnp.dot, preferred_element_type=jnp.float32)
    return dot(first[0], second[0]) + dot(first[0], second[1]) + dot(first[1], second[0])


def regroup(value):
    return jnp.concatenate(
        [
            jnp.concatenate([value[:S, :S], value[S:, :S]], axis=1),
            jnp.concatenate([value[:S, S:], value[S:, S:]], axis=1),
        ],
        axis=0,
    )


def cut(block, row, column):
    height = block.shape[0]
    lane = lax.broadcasted_iota(jnp.int32, (height, 128), 1)
    turned = [pltpu.roll(block[:, k * 128 : k * 128 + 128], 128 - column, 1) for k in range(3)]
    block = jnp.concatenate(
        [jnp.where(lane < 128 - column, turned[k], turned[k + 1]) for k in range(2)], axis=1
    )
    turned = pltpu.roll(block.reshape(height // 8, 8, S), 8 - row, 1)
    within = lax.broadcasted_iota(jnp.int32, (height // 8 - 1, 8, S), 1)
    return jnp.where(within < 8 - row, turned[:-1], turned[1:]).reshape(height - 8, S)


def placed(value, row, column):
    turned = pltpu.roll(value.reshape(S // 8, 8, S), row, 1)
    gap = jnp.zeros((1, 8, S), jnp.float32)
    within = lax.broadcasted_iota(jnp.int32, (S // 8 + 1, 8, S), 1)
    value = jnp.where(
        within < row, jnp.concatenate([gap, turned], axis=0), jnp.concatenate([turned, gap], axis=0)
    ).reshape(S + 8, S)
    lane = lax.broadcasted_iota(jnp.int32, (S + 8, 128), 1)
    turned = [pltpu.roll(value[:, k * 128 : k * 128 + 128], column, 1) for k in range(2)]
    return jnp.concatenate(
        [
            jnp.where(lane < column, 0.0, turned[0]),
            jnp.where(lane < column, turned[0], turned[1]),
            jnp.where(lane < column, turned[1], 0.0),
        ],
        axis=1,
    )


def slots_kernel(
    card, own, right, below, corner_a, corner_b, probe, frames, lh, lr, rh, rr,
    top_left, top_right, bottom, keep, send, extended, total, terms,
):
    extended[:, :S, :S] = own[...]
    extended[:, :S, S:] = right[...]
    extended[:, S:, :S] = below[...]
    extended[:, S:, S:] = corner_a[...] + corner_b[...]
    total[...] = jnp.zeros_like(total)
    terms[...] = jnp.zeros_like(terms)
    blank = jnp.zeros((S, S), jnp.float32)

    def one_slot(slot, carry):
        row, column = card[0, 2 * slot], card[0, 2 * slot + 1]
        inside = lax.rem(row, 8)
        band_rows = pl.ds(pl.multiple_of(row - inside, 8), S + 8)
        fine = lax.rem(column, 128)
        band_columns = pl.ds(pl.multiple_of(column - fine, 128), 384)
        patch_real, patch_imag = (cut(extended[p, band_rows, band_columns], inside, fine) for p in range(2))
        left_table, right_table = (lh[...], lr[...]), (rh[...], rr[...])
        RC = 256
        wave = []
        for m in range(2):
            real = probe[0, m] * patch_real - probe[1, m] * patch_imag
            imag = probe[0, m] * patch_imag + probe[1, m] * patch_real
            wave.append(product(left_table, split(jnp.concatenate([real, imag], axis=0))))
        back = [[], []]
        for at in range(0, S, RC):
            part = slice(at, at + RC)
            far = [
                jnp.concatenate([wave[m][at : at + RC], wave[m][S + at : S + at + RC]], axis=1)
                for m in range(2)
            ]
            far = product(split(jnp.concatenate(far, axis=0)), right_table)
            power = far[:RC] * far[:RC] + far[RC:] * far[RC:]
            power = power[:, :S] + power[:, S:]
            change = jnp.sqrt(frames[slot, part]) / jnp.sqrt(power + 1.0) - 1.0
            change = jnp.concatenate([change, change], axis=0)
            swapped = jnp.concatenate([far[:, S:] * change, far[:, :S] * change], axis=1)
            chunk = product(split(swapped), right_table)
            for m in range(2):
                back[m].append(chunk[m * RC : m * RC + RC])
        object_real, object_imag = blank, blank
        for m in range(2):
            whole = jnp.concatenate([c[:, :S] for c in back[m]] + [c[:, S:] for c in back[m]], axis=0)
            chi = product(left_table, split(whole))
            chi_imag, chi_real = chi[:S], chi[S:]
            object_real += probe[0, m] * chi_real + probe[1, m] * chi_imag
            object_imag += probe[0, m] * chi_imag - probe[1, m] * chi_real
            terms[m] += patch_real * chi_real + patch_imag * chi_imag
            terms[2 + m] += patch_real * chi_imag - patch_imag * chi_real
        terms[4] += patch_real * patch_real + patch_imag * patch_imag
        light = blank
        for m in range(2):
            light += probe[0, m] * probe[0, m] + probe[1, m] * probe[1, m]
        for plane, value in enumerate((object_real, object_imag, light)):
            total[plane, band_rows, band_columns] += placed(value, inside, fine)
        return carry

    lax.fori_loop(0, card[0, COUNT], one_slot, 0)
    rows = S // QUARTERS
    for q in range(QUARTERS):
        upper, lower = slice(q * rows, (q + 1) * rows), slice(S + q * rows, S + (q + 1) * rows)
        top_left[q] = total[:, upper, :S]
        top_right[q] = total[:, upper, S:]
        bottom[0, q] = total[:, lower, :S]
        bottom[1, q] = total[:, lower, S:]
    chunks, _, height, _ = keep.shape
    core = lax.axis_index("core")
    for chunk in range(chunks):
        mine = pl.multiple_of(core * (S // 2) + chunk * height, height)
        other = pl.multiple_of((1 - core) * (S // 2) + chunk * height, height)
        for plane in range(5):
            keep[chunk, plane] = terms[plane, pl.ds(mine, height), :]
            send[chunk, plane] = terms[plane, pl.ds(other, height), :]


def run_slots(card, blocks, probe, frames, chunks):
    height = S // 2 // chunks
    f32 = jnp.float32
    quarter = (QUARTERS, 3, S // QUARTERS, S)
    vmem = pl.BlockSpec(memory_space=pltpu.VMEM)
    return pl.pallas_call(
        slots_kernel,
        out_shape=(
            jax.ShapeDtypeStruct(quarter, f32),
            jax.ShapeDtypeStruct(quarter, f32),
            jax.ShapeDtypeStruct((2, *quarter), f32),
            jax.ShapeDtypeStruct((chunks, 5, height, S), f32),
            jax.ShapeDtypeStruct((chunks, 5, height, S), f32),
        ),
        in_specs=[pl.BlockSpec(memory_space=pltpu.SMEM), *[vmem] * 11],
        out_specs=[vmem] * 5,
        scratch_shapes=[
            pltpu.VMEM((2, 2 * S, 2 * S), f32),
            pltpu.VMEM((3, 2 * S, 2 * S), f32),
            pltpu.VMEM((5, S, S), f32),
        ],
        compiler_params=pltpu.CompilerParams(vmem_limit_bytes=54 * 1024 * 1024),
        name="slots",
    )(card, *blocks, probe, frames, *(jnp.asarray(t) for t in tables()))


def moved(block, tiles_by, bands_by):
    tiles, bands = lax.axis_size(TILE), lax.axis_size("band")
    route = [
        (t * bands + b, (t + tiles_by) * bands + b + bands_by)
        for t in range(tiles)
        for b in range(bands)
        if t + tiles_by in range(tiles) and b + bands_by in range(bands)
    ]
    return lax.ppermute(block, (*TILE, "band"), route)


def across_cores(block):
    return lax.ppermute(block, "core", [(0, 1), (1, 0)])


def across_posts(block, bits):
    return lax.ppermute(block, "pos", [(p, p ^ bits) for p in range(QUARTERS)])


def exchanged(block, axes):
    return lax.all_to_all(block, axes, 0, 0)


def shared(block, axes):
    return exchanged(jnp.broadcast_to(block, (lax.axis_size(axes), *block.shape)), axes)


def corners(right, below):
    tiles, bands = lax.axis_size(TILE), lax.axis_size("band")
    across = [(t * bands + b, t * bands + b - 1) for t in range(1, tiles, 2) for b in range(1, bands)]
    return lax.ppermute(below, (*TILE, "band"), across), lax.ppermute(right, "core", [(1, 0)])


def on_device(object_planes, probe_planes, patterns, offsets, counts):
    core, band, post = (lax.axis_index(name) for name in ("core", "band", "pos"))
    bands, posts = lax.axis_size("band"), lax.axis_size("pos")
    plane = ("band", "pos")
    chunks = bands * posts
    right = moved(object_planes, 0, -1)
    below = moved(object_planes, -1, 0)
    card = jnp.pad(jnp.concatenate([offsets.reshape(6), counts.reshape(1)])[None], ((0, 0), (0, 121)))
    corner_a, corner_b = corners(right, below)
    top_left, top_right, bottom, keep, send = run_slots(
        card, (object_planes, right, below, corner_a, corner_b),
        probe_planes, patterns[0, 0, 0], chunks,
    )

    from_above = moved(bottom, 1, 0)
    terms = keep + across_cores(send)
    terms = jnp.sum(exchanged(terms, plane), axis=0)
    terms, from_above = lax.optimization_barrier((terms, from_above))
    from_left = moved(top_right + from_above[1], 0, 1)
    terms = jnp.sum(shared(terms, "z_low"), axis=0)
    tile_sum = top_left + from_above[0] + from_left
    pieces = [lax.dynamic_index_in_dim(tile_sum, post ^ k, 0, keepdims=False) for k in range(QUARTERS)]
    pieces = [pieces[0], *(across_posts(pieces[k], k) for k in range(1, QUARTERS))]
    terms = jnp.sum(shared(terms, "z_high"), axis=0)

    rows = S // QUARTERS
    own_rows = lax.dynamic_slice_in_dim(object_planes, post * rows, rows, 1)
    pieces = sum(pieces[1:], pieces[0])
    own_rows = own_rows + pieces[:2] / (pieces[2] + 1.0)
    object_new = jnp.zeros_like(object_planes)
    for k in range(QUARTERS):
        piece = across_posts(own_rows, k) if k else own_rows
        object_new = lax.dynamic_update_slice_in_dim(object_new, piece, (post ^ k) * rows, 1)

    height = S // 2 // chunks
    place = core * (S // 2) + (band * posts + post) * height
    own_probe = lax.dynamic_slice_in_dim(probe_planes.reshape(4, S, S), place, height, 1)
    own_probe = own_probe + terms[:4] / (terms[4] + 1.0)
    mine = shared(own_probe, plane).transpose(1, 0, 2, 3).reshape(4, S // 2, S)
    probe_new = jnp.zeros((4, S, S), jnp.float32)
    for half, at in ((mine, core), (across_cores(mine), 1 - core)):
        probe_new = lax.dynamic_update_slice_in_dim(probe_new, half, at * (S // 2), 1)
    return (object_new, probe_new.reshape(probe_planes.shape))


def solution(mesh):
    tiles, bands, posts = mesh.devices.shape
    low = min(4, tiles // 2)
    devices = mesh.devices.reshape(tiles // 2 // low, low, 2, bands, posts)
    mesh = jax.sharding.Mesh(devices, (*TILE, "band", "pos"))
    in_specs = (
        P(None, TILE, "band"),
        P(),
        P(TILE, "band", "pos", None, None, None),
        P(TILE, "band", "pos", None, None),
        P(TILE, "band", "pos"),
    )
    out_specs = (P(None, TILE, "band"), P())
    return jax.shard_map(
        on_device, mesh=mesh, in_specs=in_specs, out_specs=out_specs, check_vma=False
    )
```

```python
import functools
import math

import jax
import jax.numpy as jnp
import ml_dtypes
import numpy as np
from jax import lax
from jax.experimental import pallas as pl
from jax.experimental.pallas import tpu as pltpu
from jax.sharding import PartitionSpec as P

S = 256
QUARTERS = 4
COUNT = 6
TILE = ("z_high", "z_low", "core")


def waves():
    index = np.arange(S)
    angle = (index[:, None] * index[None, :] % S) * (2.0 * math.pi / S)
    both = np.stack([np.cos(angle), np.sin(angle)]).astype(np.float32) / 16.0
    head = both.astype(ml_dtypes.bfloat16)
    return np.stack([head, (both - head.astype(np.float32)).astype(ml_dtypes.bfloat16)])


def table(cosine, sine):
    return jnp.concatenate(
        [jnp.concatenate([cosine, sine], axis=1), jnp.concatenate([-sine, cosine], axis=1)], axis=0
    )


def split(value):
    head = value.astype(jnp.bfloat16)
    return head, (value - head.astype(jnp.float32)).astype(jnp.bfloat16)


def product(first, second):
    dot = functools.partial(jnp.dot, preferred_element_type=jnp.float32)
    return dot(first[0], second[0]) + dot(first[0], second[1]) + dot(first[1], second[0])


def regroup(value):
    return jnp.concatenate(
        [
            jnp.concatenate([value[:S, :S], value[S:, :S]], axis=1),
            jnp.concatenate([value[:S, S:], value[S:, S:]], axis=1),
        ],
        axis=0,
    )


def cut(block, row, column):
    height = block.shape[0]
    lane = lax.broadcasted_iota(jnp.int32, (height, 128), 1)
    turned = [pltpu.roll(block[:, k * 128 : k * 128 + 128], 128 - column, 1) for k in range(3)]
    block = jnp.concatenate(
        [jnp.where(lane < 128 - column, turned[k], turned[k + 1]) for k in range(2)], axis=1
    )
    turned = pltpu.roll(block.reshape(height // 8, 8, S), 8 - row, 1)
    within = lax.broadcasted_iota(jnp.int32, (height // 8 - 1, 8, S), 1)
    return jnp.where(within < 8 - row, turned[:-1], turned[1:]).reshape(height - 8, S)


def placed(value, row, column):
    turned = pltpu.roll(value.reshape(S // 8, 8, S), row, 1)
    gap = jnp.zeros((1, 8, S), jnp.float32)
    within = lax.broadcasted_iota(jnp.int32, (S // 8 + 1, 8, S), 1)
    value = jnp.where(
        within < row, jnp.concatenate([gap, turned], axis=0), jnp.concatenate([turned, gap], axis=0)
    ).reshape(S + 8, S)
    lane = lax.broadcasted_iota(jnp.int32, (S + 8, 128), 1)
    turned = [pltpu.roll(value[:, k * 128 : k * 128 + 128], column, 1) for k in range(2)]
    return jnp.concatenate(
        [
            jnp.where(lane < column, 0.0, turned[0]),
            jnp.where(lane < column, turned[0], turned[1]),
            jnp.where(lane < column, turned[1], 0.0),
        ],
        axis=1,
    )


def slots_kernel(
    card, own, right, below, corner_a, corner_b, probe, roots, lh, lr,
    top_left, top_right, bottom, keep, send, extended, total, terms, rh, rr,
):
    extended[:, :S, :S] = own[...]
    extended[:, :S, S:] = right[...]
    extended[:, S:, :S] = below[...]
    extended[:, S:, S:] = corner_a[...] + corner_b[...]
    total[...] = jnp.zeros_like(total)
    terms[...] = jnp.zeros_like(terms)
    rh[...], rr[...] = regroup(lh[...]), regroup(lr[...])
    blank = jnp.zeros((S, S), jnp.float32)

    def one_slot(slot, carry):
        row, column = card[0, 2 * slot], card[0, 2 * slot + 1]
        inside = lax.rem(row, 8)
        band_rows = pl.ds(pl.multiple_of(row - inside, 8), S + 8)
        fine = lax.rem(column, 128)
        band_columns = pl.ds(pl.multiple_of(column - fine, 128), 384)
        patch_real, patch_imag = (cut(extended[p, band_rows, band_columns], inside, fine) for p in range(2))
        left_table, right_table = (lh[...], lr[...]), (rh[...], rr[...])
        RC = 256
        wave = []
        for m in range(2):
            real = probe[m] * patch_real - probe[2 + m] * patch_imag
            imag = probe[m] * patch_imag + probe[2 + m] * patch_real
            wave.append(product(left_table, split(jnp.concatenate([real, imag], axis=0))))
        back = [[], []]
        for at in range(0, S, RC):
            part = slice(at, at + RC)
            far = [
                jnp.concatenate([wave[m][at : at + RC], wave[m][S + at : S + at + RC]], axis=1)
                for m in range(2)
            ]
            far = product(split(jnp.concatenate(far, axis=0)), right_table)
            power = far[:RC] * far[:RC] + far[RC:] * far[RC:]
            power = power[:, :S] + power[:, S:]
            change = roots[slot, part] / jnp.sqrt(power + 1.0) - 1.0
            change = jnp.concatenate([change, change], axis=0)
            swapped = jnp.concatenate([far[:, S:] * change, far[:, :S] * change], axis=1)
            chunk = product(split(swapped), right_table)
            for m in range(2):
                back[m].append(chunk[m * RC : m * RC + RC])
        object_real, object_imag = blank, blank
        for m in range(2):
            whole = jnp.concatenate([c[:, :S] for c in back[m]] + [c[:, S:] for c in back[m]], axis=0)
            chi = product(left_table, split(whole))
            chi_imag, chi_real = chi[:S], chi[S:]
            object_real += probe[m] * chi_real + probe[2 + m] * chi_imag
            object_imag += probe[m] * chi_imag - probe[2 + m] * chi_real
            terms[m] += patch_real * chi_real + patch_imag * chi_imag
            terms[2 + m] += patch_real * chi_imag - patch_imag * chi_real
        terms[4] += patch_real * patch_real + patch_imag * patch_imag
        for plane, value in enumerate((object_real, object_imag, probe[4])):
            total[plane, band_rows, band_columns] += placed(value, inside, fine)
        return carry

    lax.fori_loop(0, card[0, COUNT], one_slot, 0)
    rows = S // QUARTERS
    for q in range(QUARTERS):
        upper, lower = slice(q * rows, (q + 1) * rows), slice(S + q * rows, S + (q + 1) * rows)
        top_left[q] = total[:, upper, :S]
        top_right[q] = total[:, upper, S:]
        bottom[0, q] = total[:, lower, :S]
        bottom[1, q] = total[:, lower, S:]
    chunks, _, height, _ = keep.shape
    core = lax.axis_index("core")
    for chunk in range(chunks):
        mine = pl.multiple_of(core * (S // 2) + chunk * height, height)
        other = pl.multiple_of((1 - core) * (S // 2) + chunk * height, height)
        for plane in range(5):
            keep[chunk, plane] = terms[plane, pl.ds(mine, height), :]
            send[chunk, plane] = terms[plane, pl.ds(other, height), :]


def run_slots(card, blocks, probe, roots, tables, chunks):
    height = S // 2 // chunks
    f32 = jnp.float32
    quarter = (QUARTERS, 3, S // QUARTERS, S)
    vmem = pl.BlockSpec(memory_space=pltpu.VMEM)
    return pl.pallas_call(
        slots_kernel,
        out_shape=(
            jax.ShapeDtypeStruct(quarter, f32),
            jax.ShapeDtypeStruct(quarter, f32),
            jax.ShapeDtypeStruct((2, *quarter), f32),
            jax.ShapeDtypeStruct((chunks, 5, height, S), f32),
            jax.ShapeDtypeStruct((chunks, 5, height, S), f32),
        ),
        in_specs=[pl.BlockSpec(memory_space=pltpu.SMEM), *[vmem] * 9],
        out_specs=[vmem] * 5,
        scratch_shapes=[
            pltpu.VMEM((2, 2 * S, 2 * S), f32),
            pltpu.VMEM((3, 2 * S, 2 * S), f32),
            pltpu.VMEM((5, S, S), f32),
            pltpu.VMEM((2 * S, 2 * S), jnp.bfloat16),
            pltpu.VMEM((2 * S, 2 * S), jnp.bfloat16),
        ],
        compiler_params=pltpu.CompilerParams(vmem_limit_bytes=40 * 1024 * 1024),
        name="slots",
    )(card, *blocks, probe, roots, *tables)


def moved(block, tiles_by, bands_by):
    tiles, bands = lax.axis_size(TILE), lax.axis_size("band")
    route = [
        (t * bands + b, (t + tiles_by) * bands + b + bands_by)
        for t in range(tiles)
        for b in range(bands)
        if t + tiles_by in range(tiles) and b + bands_by in range(bands)
    ]
    return lax.ppermute(block, (*TILE, "band"), route)


def across_cores(block):
    return lax.ppermute(block, "core", [(0, 1), (1, 0)])


def across_posts(block, bits):
    return lax.ppermute(block, "pos", [(p, p ^ bits) for p in range(QUARTERS)])


def exchanged(block, axes):
    return lax.all_to_all(block, axes, 0, 0)


def shared(block, axes):
    return exchanged(jnp.broadcast_to(block, (lax.axis_size(axes), *block.shape)), axes)


def corners(right, below):
    tiles, bands = lax.axis_size(TILE), lax.axis_size("band")
    across = [(t * bands + b, t * bands + b - 1) for t in range(1, tiles, 2) for b in range(1, bands)]
    return lax.ppermute(below, (*TILE, "band"), across), lax.ppermute(right, "core", [(1, 0)])


def on_device(object_planes, probe_planes, patterns, offsets, counts):
    core, band, post = (lax.axis_index(name) for name in ("core", "band", "pos"))
    bands, posts = lax.axis_size("band"), lax.axis_size("pos")
    plane = ("band", "pos")
    chunks = bands * posts
    right = moved(object_planes, 0, -1)
    below = moved(object_planes, -1, 0)
    card = jnp.pad(jnp.concatenate([offsets.reshape(6), counts.reshape(1)])[None], ((0, 0), (0, 121)))
    power = jnp.sum(probe_planes[0] ** 2 + probe_planes[1] ** 2, axis=0)
    probe = jnp.concatenate([probe_planes.reshape(4, S, S), power[None]])
    roots = jnp.sqrt(patterns[0, 0, 0])
    parts = lax.optimization_barrier(jnp.asarray(waves()))
    tables = (table(*parts[0]), table(*parts[1]))
    below, card, probe, roots, tables = lax.optimization_barrier((below, card, probe, roots, tables))
    corner_a, corner_b = corners(right, below)
    top_left, top_right, bottom, keep, send = run_slots(
        card, (object_planes, right, below, corner_a, corner_b),
        probe, roots, tables, chunks,
    )

    from_above = moved(bottom, 1, 0)
    terms = keep + across_cores(send)
    terms = jnp.sum(exchanged(terms, plane), axis=0)
    terms, from_above = lax.optimization_barrier((terms, from_above))
    from_left = moved(top_right + from_above[1], 0, 1)
    terms = jnp.sum(shared(terms, "z_low"), axis=0)
    tile_sum = top_left + from_above[0] + from_left
    pieces = [lax.dynamic_index_in_dim(tile_sum, post ^ k, 0, keepdims=False) for k in range(QUARTERS)]
    pieces = [pieces[0], *(across_posts(pieces[k], k) for k in range(1, QUARTERS))]
    terms = jnp.sum(shared(terms, "z_high"), axis=0)

    rows = S // QUARTERS
    own_rows = lax.dynamic_slice_in_dim(object_planes, post * rows, rows, 1)
    pieces = sum(pieces[1:], pieces[0])
    own_rows = own_rows + pieces[:2] / (pieces[2] + 1.0)
    object_new = jnp.zeros_like(object_planes)
    for k in range(QUARTERS):
        piece = across_posts(own_rows, k) if k else own_rows
        object_new = lax.dynamic_update_slice_in_dim(object_new, piece, (post ^ k) * rows, 1)

    height = S // 2 // chunks
    place = core * (S // 2) + (band * posts + post) * height
    own_probe = lax.dynamic_slice_in_dim(probe_planes.reshape(4, S, S), place, height, 1)
    own_probe = own_probe + terms[:4] / (terms[4] + 1.0)
    mine = shared(own_probe, plane).transpose(1, 0, 2, 3).reshape(4, S // 2, S)
    probe_new = jnp.zeros((4, S, S), jnp.float32)
    for half, at in ((mine, core), (across_cores(mine), 1 - core)):
        probe_new = lax.dynamic_update_slice_in_dim(probe_new, half, at * (S // 2), 1)
    return (object_new, probe_new.reshape(probe_planes.shape))


def solution(mesh):
    tiles, bands, posts = mesh.devices.shape
    low = min(4, tiles // 2)
    devices = mesh.devices.reshape(tiles // 2 // low, low, 2, bands, posts)
    mesh = jax.sharding.Mesh(devices, (*TILE, "band", "pos"))
    in_specs = (
        P(None, TILE, "band"),
        P(),
        P(TILE, "band", "pos", None, None, None),
        P(TILE, "band", "pos", None, None),
        P(TILE, "band", "pos"),
    )
    out_specs = (P(None, TILE, "band"), P())
    return jax.shard_map(
        on_device, mesh=mesh, in_specs=in_specs, out_specs=out_specs, check_vma=False
    )
```

```python
import functools
import math

import jax
import jax.numpy as jnp
import ml_dtypes
import numpy as np
from jax import lax
from jax.experimental import pallas as pl
from jax.experimental.pallas import tpu as pltpu
from jax.sharding import PartitionSpec as P

S = 256
QUARTERS = 4
COUNT = 6
TILE = ("z_high", "z_low", "core")


def tables():
    index = np.arange(S)
    angle = (index[:, None] * index[None, :] % S) * (2.0 * math.pi / S)
    cosine, sine = np.cos(angle) / 16.0, np.sin(angle) / 16.0
    three = np.stack([cosine, sine - cosine, cosine + sine]).astype(np.float32)
    head = three.astype(ml_dtypes.bfloat16)
    return head, (three - head.astype(np.float32)).astype(ml_dtypes.bfloat16)


def split(value):
    head = value.astype(jnp.bfloat16)
    return head, (value - head.astype(jnp.float32)).astype(jnp.bfloat16)


def product(first, second):
    dot = functools.partial(jnp.dot, preferred_element_type=jnp.float32)
    return dot(first[0], second[0]) + dot(first[0], second[1]) + dot(first[1], second[0])


def cut(block, row, column):
    height = block.shape[0]
    lane = lax.broadcasted_iota(jnp.int32, (height, 128), 1)
    turned = [pltpu.roll(block[:, k * 128 : k * 128 + 128], 128 - column, 1) for k in range(3)]
    block = jnp.concatenate(
        [jnp.where(lane < 128 - column, turned[k], turned[k + 1]) for k in range(2)], axis=1
    )
    turned = pltpu.roll(block.reshape(height // 8, 8, S), 8 - row, 1)
    within = lax.broadcasted_iota(jnp.int32, (height // 8 - 1, 8, S), 1)
    return jnp.where(within < 8 - row, turned[:-1], turned[1:]).reshape(height - 8, S)


def placed(value, row, column):
    turned = pltpu.roll(value.reshape(S // 8, 8, S), row, 1)
    gap = jnp.zeros((1, 8, S), jnp.float32)
    within = lax.broadcasted_iota(jnp.int32, (S // 8 + 1, 8, S), 1)
    value = jnp.where(
        within < row, jnp.concatenate([gap, turned], axis=0), jnp.concatenate([turned, gap], axis=0)
    ).reshape(S + 8, S)
    lane = lax.broadcasted_iota(jnp.int32, (S + 8, 128), 1)
    turned = [pltpu.roll(value[:, k * 128 : k * 128 + 128], column, 1) for k in range(2)]
    return jnp.concatenate(
        [
            jnp.where(lane < column, 0.0, turned[0]),
            jnp.where(lane < column, turned[0], turned[1]),
            jnp.where(lane < column, turned[1], 0.0),
        ],
        axis=1,
    )


def slots_kernel(
    card, own, right, below, corner_a, corner_b, probe, roots, head, rest,
    top_left, top_right, bottom, keep, send, extended, total, terms,
):
    extended[:, :S, :S] = own[...]
    extended[:, :S, S:] = right[...]
    extended[:, S:, :S] = below[...]
    extended[:, S:, S:] = corner_a[...] + corner_b[...]
    total[...] = jnp.zeros_like(total)
    terms[...] = jnp.zeros_like(terms)
    blank = jnp.zeros((S, S), jnp.float32)

    def one_slot(slot, carry):
        row, column = card[0, 2 * slot], card[0, 2 * slot + 1]
        inside = lax.rem(row, 8)
        band_rows = pl.ds(pl.multiple_of(row - inside, 8), S + 8)
        fine = lax.rem(column, 128)
        band_columns = pl.ds(pl.multiple_of(column - fine, 128), 384)
        patch_real, patch_imag = (cut(extended[p, band_rows, band_columns], inside, fine) for p in range(2))

        def down(real, imag):
            both, second, first = (
                product((head[k], rest[k]), split(v)) for k, v in enumerate((real + imag, imag, real))
            )
            return both + second, both - first

        def along(real, imag):
            both, second, first = (
                product(split(v), (head[k], rest[k])) for k, v in enumerate((real + imag, imag, real))
            )
            return both + second, both - first

        wave = [
            down(probe[m] * patch_real - probe[2 + m] * patch_imag, probe[m] * patch_imag + probe[2 + m] * patch_real)
            for m in range(2)
        ]
        real, imag = along(*(jnp.concatenate([wave[0][k], wave[1][k]], axis=0) for k in range(2)))
        power = real * real + imag * imag
        change = roots[slot] / jnp.sqrt(power[:S] + power[S:] + 1.0) - 1.0
        change = jnp.concatenate([change, change], axis=0)
        back = along(imag * change, real * change)
        object_real, object_imag = blank, blank
        for m in range(2):
            chi_imag, chi_real = down(back[0][m * S : m * S + S], back[1][m * S : m * S + S])
            object_real += probe[m] * chi_real + probe[2 + m] * chi_imag
            object_imag += probe[m] * chi_imag - probe[2 + m] * chi_real
            terms[m] += patch_real * chi_real + patch_imag * chi_imag
            terms[2 + m] += patch_real * chi_imag - patch_imag * chi_real
        terms[4] += patch_real * patch_real + patch_imag * patch_imag
        for plane, value in enumerate((object_real, object_imag, probe[4])):
            total[plane, band_rows, band_columns] += placed(value, inside, fine)
        return carry

    lax.fori_loop(0, card[0, COUNT], one_slot, 0)
    rows = S // QUARTERS
    for q in range(QUARTERS):
        upper, lower = slice(q * rows, (q + 1) * rows), slice(S + q * rows, S + (q + 1) * rows)
        top_left[q] = total[:, upper, :S]
        top_right[q] = total[:, upper, S:]
        bottom[0, q] = total[:, lower, :S]
        bottom[1, q] = total[:, lower, S:]
    chunks, _, height, _ = keep.shape
    core = lax.axis_index("core")
    for chunk in range(chunks):
        mine = pl.multiple_of(core * (S // 2) + chunk * height, height)
        other = pl.multiple_of((1 - core) * (S // 2) + chunk * height, height)
        for plane in range(5):
            keep[chunk, plane] = terms[plane, pl.ds(mine, height), :]
            send[chunk, plane] = terms[plane, pl.ds(other, height), :]


def run_slots(card, blocks, probe, roots, parts, chunks):
    height = S // 2 // chunks
    f32 = jnp.float32
    quarter = (QUARTERS, 3, S // QUARTERS, S)
    vmem = pl.BlockSpec(memory_space=pltpu.VMEM)
    return pl.pallas_call(
        slots_kernel,
        out_shape=(
            jax.ShapeDtypeStruct(quarter, f32),
            jax.ShapeDtypeStruct(quarter, f32),
            jax.ShapeDtypeStruct((2, *quarter), f32),
            jax.ShapeDtypeStruct((chunks, 5, height, S), f32),
            jax.ShapeDtypeStruct((chunks, 5, height, S), f32),
        ),
        in_specs=[pl.BlockSpec(memory_space=pltpu.SMEM), *[vmem] * 9],
        out_specs=[vmem] * 5,
        scratch_shapes=[
            pltpu.VMEM((2, 2 * S, 2 * S), f32),
            pltpu.VMEM((3, 2 * S, 2 * S), f32),
            pltpu.VMEM((5, S, S), f32),
        ],
        compiler_params=pltpu.CompilerParams(vmem_limit_bytes=40 * 1024 * 1024),
        name="slots",
    )(card, *blocks, probe, roots, *parts)


def moved(block, tiles_by, bands_by):
    tiles, bands = lax.axis_size(TILE), lax.axis_size("band")
    route = [
        (t * bands + b, (t + tiles_by) * bands + b + bands_by)
        for t in range(tiles)
        for b in range(bands)
        if t + tiles_by in range(tiles) and b + bands_by in range(bands)
    ]
    return lax.ppermute(block, (*TILE, "band"), route)


def across_cores(block):
    return lax.ppermute(block, "core", [(0, 1), (1, 0)])


def across_posts(block, bits):
    return lax.ppermute(block, "pos", [(p, p ^ bits) for p in range(QUARTERS)])


def exchanged(block, axes):
    return lax.all_to_all(block, axes, 0, 0)


def shared(block, axes):
    return exchanged(jnp.broadcast_to(block, (lax.axis_size(axes), *block.shape)), axes)


def corners(right, below):
    tiles, bands = lax.axis_size(TILE), lax.axis_size("band")
    across = [(t * bands + b, t * bands + b - 1) for t in range(1, tiles, 2) for b in range(1, bands)]
    return lax.ppermute(below, (*TILE, "band"), across), lax.ppermute(right, "core", [(1, 0)])


def on_device(object_planes, probe_planes, patterns, offsets, counts):
    core, band, post = (lax.axis_index(name) for name in ("core", "band", "pos"))
    bands, posts = lax.axis_size("band"), lax.axis_size("pos")
    plane = ("band", "pos")
    chunks = bands * posts
    right = moved(object_planes, 0, -1)
    below = moved(object_planes, -1, 0)
    card = jnp.pad(jnp.concatenate([offsets.reshape(6), counts.reshape(1)])[None], ((0, 0), (0, 121)))
    power = jnp.sum(probe_planes[0] ** 2 + probe_planes[1] ** 2, axis=0)
    probe = jnp.concatenate([probe_planes.reshape(4, S, S), power[None]])
    roots = jnp.sqrt(patterns[0, 0, 0])
    parts = tuple(jnp.asarray(part) for part in tables())
    below, card, probe, roots = lax.optimization_barrier((below, card, probe, roots))
    corner_a, corner_b = corners(right, below)
    top_left, top_right, bottom, keep, send = run_slots(
        card, (object_planes, right, below, corner_a, corner_b),
        probe, roots, parts, chunks,
    )

    from_above = moved(bottom, 1, 0)
    terms = keep + across_cores(send)
    terms = jnp.sum(exchanged(terms, plane), axis=0)
    terms, from_above = lax.optimization_barrier((terms, from_above))
    from_left = moved(top_right + from_above[1], 0, 1)
    terms = jnp.sum(shared(terms, "z_low"), axis=0)
    tile_sum = top_left + from_above[0] + from_left
    pieces = [lax.dynamic_index_in_dim(tile_sum, post ^ k, 0, keepdims=False) for k in range(QUARTERS)]
    pieces = [pieces[0], *(across_posts(pieces[k], k) for k in range(1, QUARTERS))]
    terms = jnp.sum(shared(terms, "z_high"), axis=0)

    rows = S // QUARTERS
    own_rows = lax.dynamic_slice_in_dim(object_planes, post * rows, rows, 1)
    pieces = sum(pieces[1:], pieces[0])
    own_rows = own_rows + pieces[:2] / (pieces[2] + 1.0)
    object_new = jnp.zeros_like(object_planes)
    for k in range(QUARTERS):
        piece = across_posts(own_rows, k) if k else own_rows
        object_new = lax.dynamic_update_slice_in_dim(object_new, piece, (post ^ k) * rows, 1)

    height = S // 2 // chunks
    place = core * (S // 2) + (band * posts + post) * height
    own_probe = lax.dynamic_slice_in_dim(probe_planes.reshape(4, S, S), place, height, 1)
    own_probe = own_probe + terms[:4] / (terms[4] + 1.0)
    mine = shared(own_probe, plane).transpose(1, 0, 2, 3).reshape(4, S // 2, S)
    probe_new = jnp.zeros((4, S, S), jnp.float32)
    for half, at in ((mine, core), (across_cores(mine), 1 - core)):
        probe_new = lax.dynamic_update_slice_in_dim(probe_new, half, at * (S // 2), 1)
    return (object_new, probe_new.reshape(probe_planes.shape))


def solution(mesh):
    tiles, bands, posts = mesh.devices.shape
    low = min(4, tiles // 2)
    devices = mesh.devices.reshape(tiles // 2 // low, low, 2, bands, posts)
    mesh = jax.sharding.Mesh(devices, (*TILE, "band", "pos"))
    in_specs = (
        P(None, TILE, "band"),
        P(),
        P(TILE, "band", "pos", None, None, None),
        P(TILE, "band", "pos", None, None),
        P(TILE, "band", "pos"),
    )
    out_specs = (P(None, TILE, "band"), P())
    return jax.shard_map(
        on_device, mesh=mesh, in_specs=in_specs, out_specs=out_specs, check_vma=False
    )
```

```python
import functools
import math

import jax
import jax.numpy as jnp
import ml_dtypes
import numpy as np
from jax import lax
from jax.experimental import pallas as pl
from jax.experimental.pallas import tpu as pltpu
from jax.sharding import PartitionSpec as P

S = 256
QUARTERS = 4
PARTNERS = (0, 1, 3, 2)
COUNT = 6
TILE = ("z_high", "z_low", "core")


def tables():
    index = np.arange(S)
    angle = (index[:, None] * index[None, :] % S) * (2.0 * math.pi / S)
    cosine, sine = np.cos(angle) / 16.0, np.sin(angle) / 16.0
    three = np.stack([cosine, sine - cosine, cosine + sine]).astype(np.float32)
    head = three.astype(ml_dtypes.bfloat16)
    return head, (three - head.astype(np.float32)).astype(ml_dtypes.bfloat16)


def split(value):
    head = value.astype(jnp.bfloat16)
    return head, (value - head.astype(jnp.float32)).astype(jnp.bfloat16)


def product(first, second):
    dot = functools.partial(jnp.dot, preferred_element_type=jnp.float32)
    return dot(first[0], second[0]) + dot(first[0], second[1]) + dot(first[1], second[0])


def cut(block, row, column):
    height = block.shape[0]
    lane = lax.broadcasted_iota(jnp.int32, (height, 128), 1)
    turned = [pltpu.roll(block[:, k * 128 : k * 128 + 128], 128 - column, 1) for k in range(3)]
    block = jnp.concatenate(
        [jnp.where(lane < 128 - column, turned[k], turned[k + 1]) for k in range(2)], axis=1
    )
    turned = pltpu.roll(block.reshape(height // 8, 8, S), 8 - row, 1)
    within = lax.broadcasted_iota(jnp.int32, (height // 8 - 1, 8, S), 1)
    return jnp.where(within < 8 - row, turned[:-1], turned[1:]).reshape(height - 8, S)


def placed(value, row, column):
    turned = pltpu.roll(value.reshape(S // 8, 8, S), row, 1)
    gap = jnp.zeros((1, 8, S), jnp.float32)
    within = lax.broadcasted_iota(jnp.int32, (S // 8 + 1, 8, S), 1)
    value = jnp.where(
        within < row, jnp.concatenate([gap, turned], axis=0), jnp.concatenate([turned, gap], axis=0)
    ).reshape(S + 8, S)
    lane = lax.broadcasted_iota(jnp.int32, (S + 8, 128), 1)
    turned = [pltpu.roll(value[:, k * 128 : k * 128 + 128], column, 1) for k in range(2)]
    return jnp.concatenate(
        [
            jnp.where(lane < column, 0.0, turned[0]),
            jnp.where(lane < column, turned[0], turned[1]),
            jnp.where(lane < column, turned[1], 0.0),
        ],
        axis=1,
    )


def slots_kernel(
    card, own, right, below, corner_a, corner_b, probe, roots, head, rest,
    top_left, top_right, bottom, keep, send, extended, total, terms,
):
    extended[:, :S, :S] = own[...]
    extended[:, :S, S:] = right[...]
    extended[:, S:, :S] = below[...]
    extended[:, S:, S:] = corner_a[...] + corner_b[...]
    total[...] = jnp.zeros_like(total)
    terms[...] = jnp.zeros_like(terms)
    blank = jnp.zeros((S, S), jnp.float32)

    def one_slot(slot, carry):
        row, column = card[0, 2 * slot], card[0, 2 * slot + 1]
        inside = lax.rem(row, 8)
        band_rows = pl.ds(pl.multiple_of(row - inside, 8), S + 8)
        fine = lax.rem(column, 128)
        band_columns = pl.ds(pl.multiple_of(column - fine, 128), 384)
        patch_real, patch_imag = (cut(extended[p, band_rows, band_columns], inside, fine) for p in range(2))

        def down(real, imag):
            both, second, first = (
                product((head[k], rest[k]), split(v)) for k, v in enumerate((real + imag, imag, real))
            )
            return both + second, both - first

        def along(real, imag):
            both, second, first = (
                product(split(v), (head[k], rest[k])) for k, v in enumerate((real + imag, imag, real))
            )
            return both + second, both - first

        wave = [
            down(probe[m] * patch_real - probe[2 + m] * patch_imag, probe[m] * patch_imag + probe[2 + m] * patch_real)
            for m in range(2)
        ]
        real, imag = along(*(jnp.concatenate([wave[0][k], wave[1][k]], axis=0) for k in range(2)))
        power = real * real + imag * imag
        change = roots[slot] / jnp.sqrt(power[:S] + power[S:] + 1.0) - 1.0
        change = jnp.concatenate([change, change], axis=0)
        back = along(imag * change, real * change)
        object_real, object_imag = blank, blank
        for m in range(2):
            chi_imag, chi_real = down(back[0][m * S : m * S + S], back[1][m * S : m * S + S])
            object_real += probe[m] * chi_real + probe[2 + m] * chi_imag
            object_imag += probe[m] * chi_imag - probe[2 + m] * chi_real
            terms[m] += patch_real * chi_real + patch_imag * chi_imag
            terms[2 + m] += patch_real * chi_imag - patch_imag * chi_real
        terms[4] += patch_real * patch_real + patch_imag * patch_imag
        for plane, value in enumerate((object_real, object_imag, probe[4])):
            total[plane, band_rows, band_columns] += placed(value, inside, fine)
        return carry

    lax.fori_loop(0, card[0, COUNT], one_slot, 0)
    rows = S // QUARTERS
    for q in range(QUARTERS):
        upper, lower = slice(q * rows, (q + 1) * rows), slice(S + q * rows, S + (q + 1) * rows)
        top_left[q] = total[:, upper, :S]
        top_right[q] = total[:, upper, S:]
        bottom[0, q] = total[:, lower, :S]
        bottom[1, q] = total[:, lower, S:]
    chunks, _, height, _ = keep.shape
    core = lax.axis_index("core")
    for chunk in range(chunks):
        mine = pl.multiple_of(core * (S // 2) + chunk * height, height)
        other = pl.multiple_of((1 - core) * (S // 2) + chunk * height, height)
        for plane in range(5):
            keep[chunk, plane] = terms[plane, pl.ds(mine, height), :]
            send[chunk, plane] = terms[plane, pl.ds(other, height), :]


def run_slots(card, blocks, probe, roots, parts, chunks):
    height = S // 2 // chunks
    f32 = jnp.float32
    quarter = (QUARTERS, 3, S // QUARTERS, S)
    vmem = pl.BlockSpec(memory_space=pltpu.VMEM)
    return pl.pallas_call(
        slots_kernel,
        out_shape=(
            jax.ShapeDtypeStruct(quarter, f32),
            jax.ShapeDtypeStruct(quarter, f32),
            jax.ShapeDtypeStruct((2, *quarter), f32),
            jax.ShapeDtypeStruct((chunks, 5, height, S), f32),
            jax.ShapeDtypeStruct((chunks, 5, height, S), f32),
        ),
        in_specs=[pl.BlockSpec(memory_space=pltpu.SMEM), *[vmem] * 9],
        out_specs=[vmem] * 5,
        scratch_shapes=[
            pltpu.VMEM((2, 2 * S, 2 * S), f32),
            pltpu.VMEM((3, 2 * S, 2 * S), f32),
            pltpu.VMEM((5, S, S), f32),
        ],
        compiler_params=pltpu.CompilerParams(vmem_limit_bytes=40 * 1024 * 1024),
        name="slots",
    )(card, *blocks, probe, roots, *parts)


def moved(block, tiles_by, bands_by):
    tiles, bands = lax.axis_size(TILE), lax.axis_size("band")
    route = [
        (t * bands + b, (t + tiles_by) * bands + b + bands_by)
        for t in range(tiles)
        for b in range(bands)
        if t + tiles_by in range(tiles) and b + bands_by in range(bands)
    ]
    return lax.ppermute(block, (*TILE, "band"), route)


def across_cores(block):
    return lax.ppermute(block, "core", [(0, 1), (1, 0)])


def across_posts(block, bits):
    return lax.ppermute(block, "pos", [(p, p ^ bits) for p in range(QUARTERS)])


def exchanged(block, axes):
    return lax.all_to_all(block, axes, 0, 0)


def shared(block, axes):
    return exchanged(jnp.broadcast_to(block, (lax.axis_size(axes), *block.shape)), axes)


def corners(right, below):
    tiles, bands = lax.axis_size(TILE), lax.axis_size("band")
    across = [(t * bands + b, t * bands + b - 1) for t in range(1, tiles, 2) for b in range(1, bands)]
    return lax.ppermute(below, (*TILE, "band"), across), lax.ppermute(right, "core", [(1, 0)])


def on_device(object_planes, probe_planes, patterns, offsets, counts):
    core, band, post = (lax.axis_index(name) for name in ("core", "band", "pos"))
    bands, posts = lax.axis_size("band"), lax.axis_size("pos")
    plane = ("band", "pos")
    chunks = bands * posts
    right = moved(object_planes, 0, -1)
    below = moved(object_planes, -1, 0)
    card = jnp.pad(jnp.concatenate([offsets.reshape(6), counts.reshape(1)])[None], ((0, 0), (0, 121)))
    power = jnp.sum(probe_planes[0] ** 2 + probe_planes[1] ** 2, axis=0)
    probe = jnp.concatenate([probe_planes.reshape(4, S, S), power[None]])
    roots = jnp.sqrt(patterns[0, 0, 0])
    parts = tuple(jnp.asarray(part) for part in tables())
    below, card, probe, roots = lax.optimization_barrier((below, card, probe, roots))
    corner_a, corner_b = corners(right, below)
    top_left, top_right, bottom, keep, send = run_slots(
        card, (object_planes, right, below, corner_a, corner_b),
        probe, roots, parts, chunks,
    )

    from_above = moved(bottom, 1, 0)
    terms = keep + across_cores(send)
    terms = jnp.sum(exchanged(terms, plane), axis=0)
    terms, from_above = lax.optimization_barrier((terms, from_above))
    from_left = moved(top_right + from_above[1], 0, 1)
    terms = jnp.sum(shared(terms, "z_low"), axis=0)
    tile_sum = top_left + from_above[0] + from_left
    pieces = [lax.dynamic_index_in_dim(tile_sum, post ^ k, 0, keepdims=False) for k in PARTNERS]
    pieces = [pieces[0], *(across_posts(piece, k) for piece, k in zip(pieces[1:], PARTNERS[1:]))]
    terms = jnp.sum(shared(terms, "z_high"), axis=0)

    rows = S // QUARTERS
    own_rows = lax.dynamic_slice_in_dim(object_planes, post * rows, rows, 1)
    pieces = sum(pieces[1:], pieces[0])
    own_rows = own_rows + pieces[:2] / (pieces[2] + 1.0)
    object_new = jnp.zeros_like(object_planes)
    for k in PARTNERS:
        piece = across_posts(own_rows, k) if k else own_rows
        object_new = lax.dynamic_update_slice_in_dim(object_new, piece, (post ^ k) * rows, 1)

    height = S // 2 // chunks
    place = core * (S // 2) + (band * posts + post) * height
    own_probe = lax.dynamic_slice_in_dim(probe_planes.reshape(4, S, S), place, height, 1)
    own_probe = own_probe + terms[:4] / (terms[4] + 1.0)
    mine = shared(own_probe, plane).transpose(1, 0, 2, 3).reshape(4, S // 2, S)
    probe_new = jnp.zeros((4, S, S), jnp.float32)
    for half, at in ((mine, core), (across_cores(mine), 1 - core)):
        probe_new = lax.dynamic_update_slice_in_dim(probe_new, half, at * (S // 2), 1)
    return (object_new, probe_new.reshape(probe_planes.shape))


def solution(mesh):
    tiles, bands, posts = mesh.devices.shape
    low = min(4, tiles // 2)
    devices = mesh.devices.reshape(tiles // 2 // low, low, 2, bands, posts)
    mesh = jax.sharding.Mesh(devices, (*TILE, "band", "pos"))
    in_specs = (
        P(None, TILE, "band"),
        P(),
        P(TILE, "band", "pos", None, None, None),
        P(TILE, "band", "pos", None, None),
        P(TILE, "band", "pos"),
    )
    out_specs = (P(None, TILE, "band"), P())
    return jax.shard_map(
        on_device, mesh=mesh, in_specs=in_specs, out_specs=out_specs, check_vma=False
    )
```

```python
import functools
import math

import jax
import jax.numpy as jnp
import ml_dtypes
import numpy as np
from jax import lax
from jax.experimental import pallas as pl
from jax.experimental.pallas import tpu as pltpu
from jax.sharding import PartitionSpec as P

S = 256
QUARTERS = 4
PARTNERS = (0, 1, 3, 2)
COUNT = 6
TILE = ("z_high", "z_low", "core")


def tables():
    index = np.arange(S)
    angle = (index[:, None] * index[None, :] % S) * (2.0 * math.pi / S)
    cosine, sine = np.cos(angle) / 16.0, np.sin(angle) / 16.0
    three = np.stack([cosine, sine - cosine, cosine + sine]).astype(np.float32)
    head = three.astype(ml_dtypes.bfloat16)
    return head, (three - head.astype(np.float32)).astype(ml_dtypes.bfloat16)


def split(value):
    head = value.astype(jnp.bfloat16)
    return head, (value - head.astype(jnp.float32)).astype(jnp.bfloat16)


def product(first, second):
    dot = functools.partial(jnp.dot, preferred_element_type=jnp.float32)
    return dot(first[0], second[0]) + dot(first[0], second[1]) + dot(first[1], second[0])


def cut(block, row, column):
    height = block.shape[0]
    lane = lax.broadcasted_iota(jnp.int32, (height, 128), 1)
    turned = [pltpu.roll(block[:, k * 128 : k * 128 + 128], 128 - column, 1) for k in range(3)]
    block = jnp.concatenate(
        [jnp.where(lane < 128 - column, turned[k], turned[k + 1]) for k in range(2)], axis=1
    )
    turned = pltpu.roll(block.reshape(height // 8, 8, S), 8 - row, 1)
    within = lax.broadcasted_iota(jnp.int32, (height // 8 - 1, 8, S), 1)
    return jnp.where(within < 8 - row, turned[:-1], turned[1:]).reshape(height - 8, S)


def placed(value, row, column):
    turned = pltpu.roll(value.reshape(S // 8, 8, S), row, 1)
    gap = jnp.zeros((1, 8, S), jnp.float32)
    within = lax.broadcasted_iota(jnp.int32, (S // 8 + 1, 8, S), 1)
    value = jnp.where(
        within < row, jnp.concatenate([gap, turned], axis=0), jnp.concatenate([turned, gap], axis=0)
    ).reshape(S + 8, S)
    lane = lax.broadcasted_iota(jnp.int32, (S + 8, 128), 1)
    turned = [pltpu.roll(value[:, k * 128 : k * 128 + 128], column, 1) for k in range(2)]
    return jnp.concatenate(
        [
            jnp.where(lane < column, 0.0, turned[0]),
            jnp.where(lane < column, turned[0], turned[1]),
            jnp.where(lane < column, turned[1], 0.0),
        ],
        axis=1,
    )


def slots_kernel(
    card, own, right, below, corner_a, corner_b, probe, roots, head, rest,
    top_left, top_right, bottom, keep, send, extended, total, terms,
):
    extended[:, :S, :S] = own[...]
    extended[:, :S, S:] = right[...]
    extended[:, S:, :S] = below[...]
    extended[:, S:, S:] = corner_a[...] + corner_b[...]
    total[...] = jnp.zeros_like(total)
    terms[...] = jnp.zeros_like(terms)
    blank = jnp.zeros((S, S), jnp.float32)

    def one_slot(slot, carry):
        row, column = card[0, 2 * slot], card[0, 2 * slot + 1]
        inside = lax.rem(row, 8)
        band_rows = pl.ds(pl.multiple_of(row - inside, 8), S + 8)
        fine = lax.rem(column, 128)
        band_columns = pl.ds(pl.multiple_of(column - fine, 128), 384)
        patch_real, patch_imag = (cut(extended[p, band_rows, band_columns], inside, fine) for p in range(2))

        def down(real, imag):
            both, second, first = (
                product((head[k], rest[k]), split(v)) for k, v in enumerate((real + imag, imag, real))
            )
            return both + second, both - first

        def along(real, imag):
            both, second, first = (
                product(split(v), (head[k], rest[k])) for k, v in enumerate((real + imag, imag, real))
            )
            return both + second, both - first

        wave = [
            down(probe[m] * patch_real - probe[2 + m] * patch_imag, probe[m] * patch_imag + probe[2 + m] * patch_real)
            for m in range(2)
        ]
        real, imag = along(*(jnp.concatenate([wave[0][k], wave[1][k]], axis=0) for k in range(2)))
        power = real * real + imag * imag
        change = roots[slot] / jnp.sqrt(power[:S] + power[S:] + 1.0) - 1.0
        change = jnp.concatenate([change, change], axis=0)
        back = along(imag * change, real * change)
        object_real, object_imag = blank, blank
        for m in range(2):
            chi_imag, chi_real = down(back[0][m * S : m * S + S], back[1][m * S : m * S + S])
            object_real += probe[m] * chi_real + probe[2 + m] * chi_imag
            object_imag += probe[m] * chi_imag - probe[2 + m] * chi_real
            terms[m] += patch_real * chi_real + patch_imag * chi_imag
            terms[2 + m] += patch_real * chi_imag - patch_imag * chi_real
        terms[4] += patch_real * patch_real + patch_imag * patch_imag
        for plane, value in enumerate((object_real, object_imag, probe[4])):
            total[plane, band_rows, band_columns] += placed(value, inside, fine)
        return carry

    lax.fori_loop(0, card[0, COUNT], one_slot, 0)
    rows = S // QUARTERS
    for q in range(QUARTERS):
        upper, lower = slice(q * rows, (q + 1) * rows), slice(S + q * rows, S + (q + 1) * rows)
        top_left[q] = total[:, upper, :S]
        top_right[q] = total[:, upper, S:]
        bottom[0, q] = total[:, lower, :S]
        bottom[1, q] = total[:, lower, S:]
    chunks, _, height, _ = keep.shape
    core = lax.axis_index("core")
    for chunk in range(chunks):
        mine = pl.multiple_of(core * (S // 2) + chunk * height, height)
        other = pl.multiple_of((1 - core) * (S // 2) + chunk * height, height)
        for plane in range(5):
            keep[chunk, plane] = terms[plane, pl.ds(mine, height), :]
            send[chunk, plane] = terms[plane, pl.ds(other, height), :]


def run_slots(card, blocks, probe, roots, parts, chunks):
    height = S // 2 // chunks
    f32 = jnp.float32
    quarter = (QUARTERS, 3, S // QUARTERS, S)
    vmem = pl.BlockSpec(memory_space=pltpu.VMEM)
    return pl.pallas_call(
        slots_kernel,
        out_shape=(
            jax.ShapeDtypeStruct(quarter, f32),
            jax.ShapeDtypeStruct(quarter, f32),
            jax.ShapeDtypeStruct((2, *quarter), f32),
            jax.ShapeDtypeStruct((chunks, 5, height, S), f32),
            jax.ShapeDtypeStruct((chunks, 5, height, S), f32),
        ),
        in_specs=[pl.BlockSpec(memory_space=pltpu.SMEM), *[vmem] * 9],
        out_specs=[vmem] * 5,
        scratch_shapes=[
            pltpu.VMEM((2, 2 * S, 2 * S), f32),
            pltpu.VMEM((3, 2 * S, 2 * S), f32),
            pltpu.VMEM((5, S, S), f32),
        ],
        compiler_params=pltpu.CompilerParams(vmem_limit_bytes=40 * 1024 * 1024),
        name="slots",
    )(card, *blocks, probe, roots, *parts)


def moved(block, tiles_by, bands_by):
    tiles, bands = lax.axis_size(TILE), lax.axis_size("band")
    route = [
        (t * bands + b, (t + tiles_by) * bands + b + bands_by)
        for t in range(tiles)
        for b in range(bands)
        if t + tiles_by in range(tiles) and b + bands_by in range(bands)
    ]
    return lax.ppermute(block, (*TILE, "band"), route)


def across_cores(block):
    return lax.ppermute(block, "core", [(0, 1), (1, 0)])


def across_posts(block, bits):
    return lax.ppermute(block, "pos", [(p, p ^ bits) for p in range(QUARTERS)])


def exchanged(block, axes):
    return lax.all_to_all(block, axes, 0, 0)


def shared(block, axes):
    return exchanged(jnp.broadcast_to(block, (lax.axis_size(axes), *block.shape)), axes)


def corners(right, below):
    tiles, bands = lax.axis_size(TILE), lax.axis_size("band")
    across = [(t * bands + b, t * bands + b - 1) for t in range(1, tiles, 2) for b in range(1, bands)]
    return lax.ppermute(below, (*TILE, "band"), across), lax.ppermute(right, "core", [(1, 0)])


def on_device(object_planes, probe_planes, patterns, offsets, counts):
    core, band, post = (lax.axis_index(name) for name in ("core", "band", "pos"))
    bands, posts = lax.axis_size("band"), lax.axis_size("pos")
    plane = ("band", "pos")
    chunks = bands * posts
    right = moved(object_planes, 0, -1)
    below = moved(object_planes, -1, 0)
    card = jnp.pad(jnp.concatenate([offsets.reshape(6), counts.reshape(1)])[None], ((0, 0), (0, 121)))
    power = jnp.sum(probe_planes[0] ** 2 + probe_planes[1] ** 2, axis=0)
    probe = jnp.concatenate([probe_planes.reshape(4, S, S), power[None]])
    roots = jnp.sqrt(patterns[0, 0, 0])
    parts = tuple(jnp.asarray(part) for part in tables())
    below, card, probe, roots = lax.optimization_barrier((below, card, probe, roots))
    corner_a, corner_b = corners(right, below)
    top_left, top_right, bottom, keep, send = run_slots(
        card, (object_planes, right, below, corner_a, corner_b),
        probe, roots, parts, chunks,
    )

    from_above = moved(bottom, 1, 0)
    terms = keep + across_cores(send)
    terms = jnp.sum(exchanged(terms, plane), axis=0)
    terms, from_above = lax.optimization_barrier((terms, from_above))
    from_left = moved(top_right + from_above[1], 0, 1)
    terms = jnp.sum(shared(terms, "z_low"), axis=0)
    tile_sum = top_left + from_above[0] + from_left
    pieces = [lax.dynamic_index_in_dim(tile_sum, post ^ k, 0, keepdims=False) for k in PARTNERS]
    pieces = [pieces[0], *(across_posts(piece, k) for piece, k in zip(pieces[1:], PARTNERS[1:]))]
    terms = jnp.sum(shared(terms, "z_high"), axis=0)

    rows = S // QUARTERS
    own_rows = lax.dynamic_slice_in_dim(object_planes, post * rows, rows, 1)
    pieces = sum(pieces[1:], pieces[0])
    own_rows = own_rows + pieces[:2] / (pieces[2] + 1.0)
    gathered = [own_rows, *(across_posts(own_rows, k) for k in PARTNERS[1:])]

    height = S // 2 // chunks
    place = core * (S // 2) + (band * posts + post) * height
    own_probe = lax.dynamic_slice_in_dim(probe_planes.reshape(4, S, S), place, height, 1)
    own_probe = own_probe + terms[:4] / (terms[4] + 1.0)
    mine = shared(own_probe, plane).transpose(1, 0, 2, 3).reshape(4, S // 2, S)
    probe_new = jnp.zeros((4, S, S), jnp.float32)
    for half, at in ((mine, core), (across_cores(mine), 1 - core)):
        probe_new = lax.dynamic_update_slice_in_dim(probe_new, half, at * (S // 2), 1)
    gathered[-1] = lax.optimization_barrier((gathered[-1], probe_new))[0]
    object_new = jnp.zeros_like(object_planes)
    for piece, k in zip(gathered, PARTNERS):
        object_new = lax.dynamic_update_slice_in_dim(object_new, piece, (post ^ k) * rows, 1)
    return (object_new, probe_new.reshape(probe_planes.shape))


def solution(mesh):
    tiles, bands, posts = mesh.devices.shape
    low = min(4, tiles // 2)
    devices = mesh.devices.reshape(tiles // 2 // low, low, 2, bands, posts)
    mesh = jax.sharding.Mesh(devices, (*TILE, "band", "pos"))
    in_specs = (
        P(None, TILE, "band"),
        P(),
        P(TILE, "band", "pos", None, None, None),
        P(TILE, "band", "pos", None, None),
        P(TILE, "band", "pos"),
    )
    out_specs = (P(None, TILE, "band"), P())
    return jax.shard_map(
        on_device, mesh=mesh, in_specs=in_specs, out_specs=out_specs, check_vma=False
    )
```
